128 devices in a mesh: lat: 8 (over z, x_lo), lon: 16 (over x_hi, y, core).
Axes of the slice: x: 4 (x_hi: 2, x_lo: 2; x = x_hi * 2 + x_lo), y: 4, z: 4, core: 2. Of those that a mesh axis runs over, the one named last changes fastest.
Arguments:
- tokens: bfloat16 [96, 192, 2, 2048], P('lat', None, None, 'lon'), may hold values from -6 to 6
- upstream: bfloat16 [96, 192, 2, 2048], P('lat', 'lon'), may hold values from -6 to 6
- qkv_weight: bfloat16 [2048, 3072], P('lon'), may hold values from -1 to 1
- out_weight: bfloat16 [1024, 2048], P('lon'), may hold values from -0.1875 to 0.1875
Outputs:
- grad_tokens: bfloat16 [96, 192, 2, 2048], P('lat', None, None, 'lon')
- grad_qkv_w: float32 [8, 2048, 3072], P('lat', 'lon')
- grad_out_w: float32 [8, 1024, 2048], P('lat', 'lon')
The draws below stay inside these ranges and needn't reach their ends.
All inputs are finite; a program needn't handle non-finite values.
Results may differ from the reference program's by a relative error of at most 0.017.
Values may be sent and summed in bfloat16 or wider, within the bound.
No kernel may reach another device: no remote copies, remote signals or barrier semaphores. Data moves between devices by JAX's collectives and lax.ppermute only.
A program may use at most 128 MiB of HBM per device.

```python
import jax
import jax.numpy as jnp
from jax import lax

D = 2048
HEADS = 16
HEAD_DIM = 64
WLAT = 12
WLON = 6
LEVELS = 2
TILE_ROWS = 12
TILE_COLS = 12
LAT = 96
LON = 192
N_LAT = 8
N_LON = 16


def draw_qkv_weight(key, part):
    key = jax.random.fold_in(key, 7)
    key_base = jax.random.fold_in(key, 0)
    inner_width = HEADS * HEAD_DIM
    drawn = jnp.clip(jax.random.normal(key_base, (D, 3 * inner_width), jnp.float32), -6.0, 6.0) * D ** (-0.5)
    return jnp.clip(drawn, -1.0, 1.0).astype(jnp.bfloat16)


def steps_of(rng, extent, cuts, least, top_value):
    gain, own = 1.0, jax.random.fold_in(rng, 6)
    for position, parts in cuts:
        heights = jnp.exp(jax.random.uniform(jax.random.fold_in(own, position), (parts,), jnp.float32, least / len(cuts), top_value / len(cuts)))
        gain = gain * jnp.repeat(heights, extent[position] // parts).reshape([-1 if axis == position else 1 for axis in range(len(extent))])
    return gain


def noise(rng, shape, deviation, reach, pieces=(), held_as=jnp.bfloat16):
    array = jax.random.normal(rng, shape, jnp.float32) * deviation
    if len(pieces) > 0:
        array = steps_of(rng, shape, pieces, -0.22, 0.18) * array
    return jnp.clip(array, min=-reach, max=reach).astype(held_as)


def setup_inputs(seed: int = 0) -> dict:
    seeds = jax.random.split(jax.random.key(seed), 5)
    return {
        "tokens": noise(seeds[0], (LAT, LON, LEVELS, D), 1.0, 6.0, ((0, 8), (3, 16))),
        "upstream": noise(seeds[1], (LAT, LON, LEVELS, D), 1.0, 6.0, ((0, 8), (1, 16))),
        "qkv_weight": draw_qkv_weight(jax.random.fold_in(seeds[4], 71), 0),
        "out_weight": noise(seeds[3], (HEADS * HEAD_DIM, D), (HEADS * HEAD_DIM) ** -0.5, 0.1875, ((0, 16),)),
    }


NEG_FILL = -1e+30
EPSILON = 1e-05

def rounded(source):
    return lax.optimization_barrier(source.astype(jnp.bfloat16))

def window_split(flat_rows, row_count, col_count):
    feature_count = flat_rows.shape[-1]
    shaped = flat_rows.reshape(row_count // WLAT, WLAT, col_count // WLON, WLON, LEVELS, feature_count)
    return shaped.transpose(0, 2, 1, 3, 4, 5).reshape(-1, WLAT * WLON * LEVELS, feature_count)

def window_merge(windowed, row_count, col_count):
    feature_count = windowed.shape[-1]
    shaped = windowed.reshape(row_count // WLAT, col_count // WLON, WLAT, WLON, LEVELS, feature_count)
    return shaped.transpose(0, 2, 1, 3, 4, 5).reshape(row_count * col_count * LEVELS, feature_count)

def attention_backward(qkv_win, grad_win, group_win):
    window_count, window_tokens = (qkv_win.shape[0], qkv_win.shape[1])
    split_qkv = qkv_win.astype(jnp.float32).reshape(window_count, window_tokens, 3, HEADS, HEAD_DIM)
    queries, key_rows, values = (split_qkv[:, :, 0], split_qkv[:, :, 1], split_qkv[:, :, 2])
    score_scale = HEAD_DIM ** (-0.5)
    scores = jnp.einsum('wqhd,wkhd->whqk', queries, key_rows) * score_scale
    same_group = group_win[:, None, :, None] == group_win[:, None, None, :]
    scores = jnp.where(same_group, scores, NEG_FILL)
    top_score = lax.optimization_barrier(jnp.max(scores, axis=-1, keepdims=True))
    expons = jnp.exp(scores - top_score)
    attention = expons / lax.optimization_barrier(jnp.sum(expons, axis=-1, keepdims=True))
    attention_b = rounded(attention).astype(jnp.float32)
    attended = rounded(jnp.einsum('whqk,wkhd->wqhd', attention_b, values))
    grad_heads = grad_win.astype(jnp.float32).reshape(window_count, window_tokens, HEADS, HEAD_DIM)
    grad_probs = jnp.einsum('wqhd,wkhd->whqk', grad_heads, values)
    row_inner = lax.optimization_barrier(jnp.sum(attention * grad_probs, axis=-1, keepdims=True))
    grad_scores = rounded(attention * (grad_probs - row_inner) * score_scale).astype(jnp.float32)
    grad_query = rounded(jnp.einsum('whqk,wkhd->wqhd', grad_scores, key_rows))
    grad_key = rounded(jnp.einsum('whqk,wqhd->wkhd', grad_scores, queries))
    grad_value = rounded(jnp.einsum('whqk,wqhd->wkhd', attention_b, grad_heads))
    grad_qkv = jnp.stack([grad_query, grad_key, grad_value], axis=2)
    grad_qkv = grad_qkv.reshape(window_count, window_tokens, 3 * HEADS * HEAD_DIM)
    return (attended.reshape(window_count, window_tokens, HEADS * HEAD_DIM), grad_qkv)

def local_pass(rolled_in, rolled_grad, first_row, total_rows, qkv_full, out_full):
    row_count, col_count = (rolled_in.shape[0], rolled_in.shape[1])
    model_width = rolled_in.shape[-1]
    values_in = rolled_in.reshape(-1, model_width).astype(jnp.float32)
    average = lax.optimization_barrier(jnp.mean(values_in, axis=-1, keepdims=True))
    centred = values_in - average
    inverse = lax.rsqrt(lax.optimization_barrier(jnp.mean(centred * centred, axis=-1, keepdims=True)) + EPSILON)
    normal_full = centred * inverse
    normed = rounded(normal_full)
    qkv_flat = rounded(jnp.dot(normed, qkv_full, preferred_element_type=jnp.float32))
    grad_flat = rolled_grad.reshape(-1, model_width)
    grad_att = rounded(lax.dot_general(grad_flat, out_full, (((1,), (1,)), ((), ())), preferred_element_type=jnp.float32))
    row_ids = first_row + jnp.arange(row_count, dtype=jnp.int32)
    groups = (row_ids >= total_rows - WLAT // 2).astype(jnp.int32)
    groups = jnp.broadcast_to(groups[:, None, None], (row_count, col_count, LEVELS)).reshape(-1, 1)
    group_win = window_split(groups, row_count, col_count)[:, :, 0]
    attended_win, grad_qkv_win = attention_backward(window_split(qkv_flat, row_count, col_count), window_split(grad_att, row_count, col_count), group_win)
    attended = window_merge(attended_win, row_count, col_count)
    grad_qkv = window_merge(grad_qkv_win, row_count, col_count)
    grad_normal = lax.dot_general(grad_qkv, qkv_full, (((1,), (1,)), ((), ())), preferred_element_type=jnp.float32)
    mean_one = lax.optimization_barrier(jnp.mean(grad_normal, axis=-1, keepdims=True))
    mean_two = lax.optimization_barrier(jnp.mean(grad_normal * normal_full, axis=-1, keepdims=True))
    grad_rolled = rounded(inverse * (grad_normal - mean_one - normal_full * mean_two)).reshape(rolled_in.shape)
    return (grad_rolled, normed, grad_qkv, attended, grad_flat)

def reference(tokens, upstream, qkv_weight, out_weight):
    half_lat = WLAT // 2
    half_lon = WLON // 2
    rolled_all = jnp.roll(tokens, (-half_lat, -half_lon), (0, 1))
    rolled_cot = jnp.roll(upstream, (-half_lat, -half_lon), (0, 1))
    tile_width = TILE_COLS * LEVELS

    def per_slab(slab_index):
        first_row = slab_index * TILE_ROWS
        slab_in = lax.dynamic_slice_in_dim(rolled_all, first_row, TILE_ROWS, 0)
        slab_grad = lax.dynamic_slice_in_dim(rolled_cot, first_row, TILE_ROWS, 0)
        grad_rolled, normed, grad_qkv, attended, grad_flat = local_pass(slab_in, slab_grad, first_row, LAT, qkv_weight, out_weight)
        normed_tiles = normed.reshape(TILE_ROWS, N_LON, tile_width, -1).astype(jnp.float32)
        gradq_tiles = grad_qkv.reshape(TILE_ROWS, N_LON, tile_width, -1).astype(jnp.float32)
        qkv_terms = jnp.einsum('rjtd,rjte->jde', normed_tiles, gradq_tiles)
        qkv_sum = lax.optimization_barrier(jnp.sum(rounded(qkv_terms).astype(jnp.float32), axis=0))
        attended_tiles = attended.reshape(TILE_ROWS, N_LON, tile_width, -1).astype(jnp.float32)
        cot_tiles = grad_flat.reshape(TILE_ROWS, N_LON, tile_width, -1).astype(jnp.float32)
        out_terms = jnp.einsum('rjtd,rjte->jde', attended_tiles, cot_tiles)
        out_sum = lax.optimization_barrier(jnp.sum(rounded(out_terms).astype(jnp.float32), axis=0))
        return (grad_rolled, qkv_sum, out_sum)
    grad_slabs, grad_qkv_w, grad_out_w = lax.map(per_slab, jnp.arange(N_LAT, dtype=jnp.int32))
    grad_rolled = grad_slabs.reshape(LAT, LON, LEVELS, D)
    restored = jnp.roll(grad_rolled, (half_lat, half_lon), (0, 1))
    grad_tokens = (upstream.astype(jnp.float32) + restored.astype(jnp.float32)).astype(jnp.bfloat16)
    return (grad_tokens, grad_qkv_w, grad_out_w)
```

```python
import functools

import jax
import jax.numpy as jnp
from jax import lax
from jax.experimental import pallas as pl
from jax.experimental.pallas import tpu as pltpu
from jax.sharding import PartitionSpec as P

HEADS = 16
HEAD_DIM = 64
WLAT = 12
WLON = 6
LEVELS = 2
WTOK = WLAT * WLON * LEVELS
TILE = 2 * WTOK
HALF = WTOK // 2

NEG_FILL = -1e30
EPSILON = 1e-05

NY = 4


def lon_of(xh, y, c):
    return (xh * NY + y) * 2 + c


COORDS = [(xh, y, c) for xh in range(2) for y in range(NY) for c in range(2)]


def swap_c(value):
    return lax.ppermute(value, "lon", [(lon_of(x, y, c), lon_of(x, y, 1 - c)) for x, y, c in COORDS])


def swap_x(value):
    return lax.ppermute(value, "lon", [(lon_of(x, y, c), lon_of(1 - x, y, c)) for x, y, c in COORDS])


def shift_y(value, by):
    return lax.ppermute(value, "lon", [(lon_of(x, y, c), lon_of(x, (y + by) % NY, c)) for x, y, c in COORDS])


def passed_along(value, axis, by):
    devices = lax.axis_size(axis)
    return lax.ppermute(value, axis, [(i, (i + by) % devices) for i in range(devices)])


def mm(a, b, dims):
    return lax.dot_general(a, b, (dims, ((), ())), preferred_element_type=jnp.float32)


def main_kernel(s_ref, x0, x1, x2, x3, u0, u1, u2, u3, w0, w1, w2, w3, o0, o1, o2, o3,
                pc_ref, px_ref, po_ref, nb_ref, dq_ref, gw_ref, wfull, wout, ub, gacc):
    t = pl.program_id(0)
    xs, us, ws, os = (x0, x1, x2, x3), (u0, u1, u2, u3), (w0, w1, w2, w3), (o0, o1, o2, o3)
    y = s_ref[1]
    split = s_ref[2]

    @pl.when(t == 0)
    def _():
        for s in range(4):
            wfull[s * 512:(s + 1) * 512, :] = ws[s][...].reshape(512, 768)
            head = lax.rem(y + 4 - s, 4)
            wout[pl.ds(pl.multiple_of(head * 64, 64), 64), :] = os[s][...]
        gacc[...] = jnp.zeros_like(gacc)

    for i in range(4):
        @pl.when(t == i)
        def _(i=i):
            ub[...] = us[i][...].reshape(TILE, 2048)

    x = jnp.concatenate(
        [xs[k][s].reshape(TILE, 128) for s in range(4) for k in range(4)], axis=1
    ).astype(jnp.float32)
    average = jnp.mean(x, axis=-1, keepdims=True)
    centred = x - average
    inverse = lax.rsqrt(jnp.mean(centred * centred, axis=-1, keepdims=True) + EPSILON)
    normal = centred * inverse
    nb = normal.astype(jnp.bfloat16)
    nb_ref[...] = nb
    qkv = mm(nb, wfull[...], ((1,), (0,))).astype(jnp.bfloat16)
    grad_att = mm(ub[...], wout[...], ((1,), (1,))).astype(jnp.bfloat16)
    scale = HEAD_DIM ** (-0.5)
    row_group = lax.broadcasted_iota(jnp.int32, (WTOK, WTOK), 0) >= HALF
    col_group = lax.broadcasted_iota(jnp.int32, (WTOK, WTOK), 1) >= HALF
    keep = (row_group == col_group) | (split == 0)
    att_rows, dqkv_rows = [], []
    for w in range(2):
        rows = slice(w * WTOK, (w + 1) * WTOK)
        att_h, dq_h, dk_h, dv_h = [], [], [], []
        for h in range(4):
            q = qkv[rows, h * 64:(h + 1) * 64]
            k = qkv[rows, 256 + h * 64:256 + (h + 1) * 64]
            v = qkv[rows, 512 + h * 64:512 + (h + 1) * 64]
            g = grad_att[rows, h * 64:(h + 1) * 64]
            scores = jnp.where(keep, mm(q, k, ((1,), (1,))) * scale, NEG_FILL)
            expons = jnp.exp(scores - jnp.max(scores, axis=-1, keepdims=True))
            attention = expons / jnp.sum(expons, axis=-1, keepdims=True)
            attention_b = attention.astype(jnp.bfloat16)
            att_h.append(mm(attention_b, v, ((1,), (0,))).astype(jnp.bfloat16))
            grad_probs = mm(g, v, ((1,), (1,)))
            weighted = attention * grad_probs
            inner = jnp.sum(weighted, axis=-1, keepdims=True)
            grad_scores = ((weighted - attention * inner) * scale).astype(jnp.bfloat16)
            dq_h.append(mm(grad_scores, k, ((1,), (0,))).astype(jnp.bfloat16))
            dk_h.append(mm(grad_scores, q, ((0,), (0,))).astype(jnp.bfloat16))
            dv_h.append(mm(attention_b, g, ((0,), (0,))).astype(jnp.bfloat16))
        att_rows.append(jnp.concatenate(att_h, axis=1))
        dqkv_rows.append(jnp.concatenate(dq_h + dk_h + dv_h, axis=1))
    attended = jnp.concatenate(att_rows, axis=0)
    dqkv = jnp.concatenate(dqkv_rows, axis=0)
    dq_ref[...] = dqkv
    gacc[...] += mm(attended, ub[...], ((0,), (0,)))
    grad_normal = mm(dqkv, wfull[...], ((1,), (1,)))
    mean_one = jnp.mean(grad_normal, axis=-1, keepdims=True)
    mean_two = jnp.mean(grad_normal * normal, axis=-1, keepdims=True)
    grad_rolled = inverse * (grad_normal - mean_one - normal * mean_two)
    for s in range(4):
        part = [grad_rolled[:, (s * 4 + k) * 128:(s * 4 + k + 1) * 128].reshape(2, WTOK, 128) for k in range(4)]
        pc_ref[0, s] = part[1].astype(jnp.bfloat16)
        pc_ref[1, s] = part[3].astype(jnp.bfloat16)
        px_ref[s] = part[2].astype(jnp.bfloat16)
        block = s_ref[3] + lax.rem(y + 4 - s, 4) * 2
        own = ub[:, pl.ds(pl.multiple_of(block * 128, 128), 128)].astype(jnp.float32)
        po_ref[s] = part[0] + own.reshape(2, WTOK, 128)

    @pl.when(t == 3)
    def _():
        for s in range(4):
            head = lax.rem(y + 4 - s, 4)
            gw_ref[s] = gacc[pl.ds(pl.multiple_of(head * 64, 64), 64), :].astype(jnp.bfloat16)


def main_pass(scalars, xs, us, ws, os):
    x_spec = pl.BlockSpec((4, 2, WTOK, 128), lambda t, s: (0, t ^ s[0], 0, 0))
    u_spec = pl.BlockSpec((2, WTOK, 2048), lambda t, s: (0, 0, 0))
    w_spec = pl.BlockSpec((4, 128, 768), lambda t, s: (0, 0, 0))
    o_spec = pl.BlockSpec((64, 2048), lambda t, s: (0, 0))
    return pl.pallas_call(
        main_kernel,
        grid_spec=pltpu.PrefetchScalarGridSpec(
            num_scalar_prefetch=1,
            grid=(4,),
            in_specs=[x_spec] * 4 + [u_spec] * 4 + [w_spec] * 4 + [o_spec] * 4,
            out_specs=[
                pl.BlockSpec((2, 4, 2, WTOK, 128), lambda t, s: (0, 0, t ^ s[0], 0, 0)),
                pl.BlockSpec((4, 2, WTOK, 128), lambda t, s: (0, t ^ s[0], 0, 0)),
                pl.BlockSpec((4, 2, WTOK, 128), lambda t, s: (0, t ^ s[0], 0, 0)),
                pl.BlockSpec((TILE, 2048), lambda t, s: (t, 0)),
                pl.BlockSpec((TILE, 768), lambda t, s: (t, 0)),
                pl.BlockSpec((4, 64, 2048), lambda t, s: (0, 0, 0)),
            ],
            scratch_shapes=[
                pltpu.VMEM((2048, 768), jnp.bfloat16),
                pltpu.VMEM((256, 2048), jnp.bfloat16),
                pltpu.VMEM((TILE, 2048), jnp.bfloat16),
                pltpu.VMEM((256, 2048), jnp.float32),
            ],
        ),
        out_shape=[
            jax.ShapeDtypeStruct((2, 4, 8, WTOK, 128), jnp.bfloat16),
            jax.ShapeDtypeStruct((4, 8, WTOK, 128), jnp.bfloat16),
            jax.ShapeDtypeStruct((4, 8, WTOK, 128), jnp.float32),
            jax.ShapeDtypeStruct((4 * TILE, 2048), jnp.bfloat16),
            jax.ShapeDtypeStruct((4 * TILE, 768), jnp.bfloat16),
            jax.ShapeDtypeStruct((4, 64, 2048), jnp.bfloat16),
        ],
        compiler_params=pltpu.CompilerParams(vmem_limit_bytes=60 * 1024 * 1024),
        cost_estimate=pl.CostEstimate(flops=11 * 10**9, bytes_accessed=30 * 10**6, transcendentals=10**6),
        name="window_pass",
    )(scalars, *xs, *us, *ws, *os)


def term_kernel(nb_ref, dq_ref, out_ref):
    out_ref[...] = mm(nb_ref[...], dq_ref[...], ((0,), (0,))).astype(out_ref.dtype)


def weight_term(nb, dqkv, s, dtype):
    return pl.pallas_call(
        term_kernel,
        grid=(1,),
        in_specs=[
            pl.BlockSpec((4 * TILE, 512), lambda i: (0, s)),
            pl.BlockSpec((4 * TILE, 768), lambda i: (0, 0)),
        ],
        out_specs=pl.BlockSpec((512, 768), lambda i: (0, 0)),
        out_shape=jax.ShapeDtypeStruct((512, 768), dtype),
        compiler_params=pltpu.CompilerParams(vmem_limit_bytes=40 * 1024 * 1024),
        cost_estimate=pl.CostEstimate(flops=9 * 10**8, bytes_accessed=4 * 10**6, transcendentals=0),
        name="weight_term",
    )(nb, dqkv)


def local(tokens, upstream, qkv_weight, out_weight):
    half_lat = WLAT // 2
    half_lon = WLON // 2
    lon = lax.axis_index("lon")
    lat = lax.axis_index("lat")
    xh, y, c = lon // 8, (lon // 2) % 4, lon % 2

    w6 = qkv_weight.reshape(128, 3, 2, 4, 2, 64).transpose(2, 4, 0, 1, 3, 5).reshape(4, 128, 768)
    group = xh * 2 + c
    pick = [lax.dynamic_index_in_dim(w6, group ^ k, 0, keepdims=False) for k in range(4)]
    from_c = swap_c(jnp.stack([pick[1], pick[3]]))
    from_x = swap_x(jnp.stack([pick[2], from_c[1]]))
    shard = jnp.concatenate([jnp.stack([pick[0], from_c[0]]), from_x])
    ws = [shard] + [shift_y(shard, s) for s in (1, 2, 3)]
    os = [out_weight] + [shift_y(out_weight, s) for s in (1, 2, 3)]

    rim = passed_along(tokens[:half_lat], "lat", -1)
    rolled = jnp.roll(jnp.concatenate([tokens[half_lat:], rim], axis=0), -half_lon, axis=1)
    rolled = rolled.reshape(12, 2, 4, 2, 2, WLON, LEVELS, 128).transpose(2, 1, 3, 4, 0, 5, 6, 7)
    rolled = rolled.reshape(4, 8, WTOK, 128)
    dest = [lax.dynamic_index_in_dim(rolled, (y + s) % 4, 0, keepdims=False) for s in range(4)]
    x_own = jnp.stack([dest[0]] + [shift_y(dest[s], s) for s in (1, 2, 3)])
    x_x = swap_x(x_own)
    xs = [x_own, swap_c(x_own), x_x, swap_c(x_x)]

    lat_rim = passed_along(upstream[:half_lat], "lat", -1)
    up = jnp.concatenate([upstream[half_lat:], lat_rim], axis=0)
    lon_rim = passed_along(up[:, :half_lon], "lon", -1)
    up = jnp.concatenate([up[:, half_lon:], lon_rim], axis=1)
    up = up.reshape(12, 2, WLON, LEVELS, 2048).transpose(1, 0, 2, 3, 4).reshape(2, WTOK, 2048)
    u_x = swap_x(up)
    us = [up, swap_c(up), u_x, swap_c(u_x)]

    last = (lat == lax.axis_size("lat") - 1).astype(jnp.int32)
    scalars = jnp.stack([group, y, last, xh * 8 + c]).astype(jnp.int32)
    part_c, part_x, part_own, nb, dqkv, gw = main_pass(scalars, xs, us, ws, os)

    terms = {}
    for s in (1, 3, 2, 0):
        term = weight_term(nb, dqkv, s, jnp.float32 if s == 0 else jnp.bfloat16)
        terms[s] = term if s == 0 else shift_y(term, -s)
    total = sum((terms[s].astype(jnp.float32) for s in (1, 2, 3)), terms[0]).reshape(4, 128, 768)
    gw_total = sum((shift_y(gw[s], -s).astype(jnp.float32) for s in (1, 2, 3)), gw[0].astype(jnp.float32))

    got_c = swap_c(part_c)
    got_x = swap_x((part_x.astype(jnp.float32) + got_c[1].astype(jnp.float32)).astype(jnp.bfloat16))
    whole = (part_own + got_c[0].astype(jnp.float32) + got_x.astype(jnp.float32)).astype(jnp.bfloat16)
    back = jnp.stack([whole[0]] + [shift_y(whole[s], -s) for s in (1, 2, 3)])
    back = jnp.stack([lax.dynamic_index_in_dim(back, (i - y + 4) % 4, 0, keepdims=False) for i in range(4)])
    back = back.reshape(4, 2, 2, 2, 12, WLON, LEVELS, 128).transpose(4, 1, 0, 2, 3, 5, 6, 7)
    back = jnp.roll(back.reshape(12, 192, LEVELS, 128), half_lon, axis=1)
    previous = passed_along(back[half_lat:], "lat", 1)
    result = jnp.concatenate([previous, back[:half_lat]], axis=0)

    total_b = total.astype(jnp.bfloat16)
    cols_x = swap_x(total_b[2:])
    cols_c = swap_c(jnp.stack([total_b[1], cols_x[1]]))
    cols = jnp.stack([total[0], cols_c[0].astype(jnp.float32), cols_x[0].astype(jnp.float32), cols_c[1].astype(jnp.float32)])
    cols = jnp.stack([lax.dynamic_index_in_dim(cols, group ^ k, 0, keepdims=False) for k in range(4)])
    grad_qkv_w = cols.reshape(2, 2, 128, 3, 4, 64).transpose(2, 3, 0, 4, 1, 5).reshape(128, 3072)
    return (result, grad_qkv_w[None], gw_total[None])


def solution(mesh):
    return jax.shard_map(
        local,
        mesh=mesh,
        in_specs=(
            P("lat", None, None, "lon"),
            P("lat", "lon", None, None),
            P("lon", None),
            P("lon", None),
        ),
        out_specs=(P("lat", None, None, "lon"), P("lat", "lon", None), P("lat", "lon", None)),
        check_vma=False,
    )
```

```python
import functools

import jax
import jax.numpy as jnp
from jax import lax
from jax.experimental import pallas as pl
from jax.experimental.pallas import tpu as pltpu
from jax.sharding import PartitionSpec as P

HEAD_DIM = 64
WLAT = 12
WLON = 6
LEVELS = 2
WTOK = WLAT * WLON * LEVELS
PAIR = 2 * WTOK
HALF = WTOK // 2
D = 2048
NY = 4
MIB = 1024 * 1024

NEG_FILL = -1e30
EPSILON = 1e-05


def lon_of(xh, y, c):
    return (xh * NY + y) * 2 + c


COORDS = [(xh, y, c) for xh in range(2) for y in range(NY) for c in range(2)]


def swap_c(value):
    return lax.ppermute(value, "lon", [(lon_of(x, y, c), lon_of(x, y, 1 - c)) for x, y, c in COORDS])


def swap_x(value):
    return lax.ppermute(value, "lon", [(lon_of(x, y, c), lon_of(1 - x, y, c)) for x, y, c in COORDS])


def shift_y(value, by):
    return lax.ppermute(value, "lon", [(lon_of(x, y, c), lon_of(x, (y + by) % NY, c)) for x, y, c in COORDS])


def passed_along(value, axis, by):
    devices = lax.axis_size(axis)
    return lax.ppermute(value, axis, [(i, (i + by) % devices) for i in range(devices)])


def mm(a, b, dims):
    return lax.dot_general(a, b, (dims, ((), ())), preferred_element_type=jnp.float32)


def shape(dims, dtype=jnp.bfloat16):
    return jax.ShapeDtypeStruct(dims, dtype)


def whole(*dims):
    return pl.BlockSpec(dims, lambda *_: (0,) * len(dims))


def weight_split_kernel(s_ref, q_ref, o_ref, w_ref, out_ref):
    group = s_ref[0] * 2 + s_ref[1]
    for xh in range(2):
        for c in range(2):
            slot = group ^ (xh * 2 + c)
            for pair in range(2):
                for part in range(3):
                    block = part * 8 + xh * 4 + pair * 2
                    lo = block * 128 + c * 64
                    w_ref[slot, pair * 3 + part] = jnp.concatenate(
                        [q_ref[:, lo:lo + 64], q_ref[:, lo + 128:lo + 192]], axis=1)
    for i in range(8):
        out_ref[i] = jnp.concatenate(
            [o_ref[:, i * 256:i * 256 + 128], o_ref[:, i * 256 + 128:i * 256 + 256]], axis=0)


def weight_split(scalars, qkv_weight, out_weight):
    return pl.pallas_call(
        weight_split_kernel,
        grid_spec=pltpu.PrefetchScalarGridSpec(
            num_scalar_prefetch=1,
            grid=(1,),
            in_specs=[whole(128, 3072), whole(64, D)],
            out_specs=[whole(4, 6, 128, 128), whole(8, 128, 128)],
        ),
        out_shape=[shape((4, 6, 128, 128)), shape((8, 128, 128))],
        cost_estimate=pl.CostEstimate(flops=0, bytes_accessed=2 * 10**6, transcendentals=0),
        name="weight_split",
    )(scalars, qkv_weight, out_weight)


def weight_join_kernel(s_ref, a_ref, b_ref, out_ref):
    group = s_ref[0] * 2 + s_ref[1]
    for xh in range(2):
        slots = [group ^ (xh * 2), group ^ (xh * 2 + 1)]
        for pair, ref in enumerate((a_ref, b_ref)):
            for part in range(3):
                left, right = ref[slots[0], part], ref[slots[1], part]
                lo = (part * 8 + xh * 4 + pair * 2) * 128
                out_ref[:, lo:lo + 128] = jnp.concatenate([left[:, :64], right[:, :64]], axis=1)
                out_ref[:, lo + 128:lo + 256] = jnp.concatenate([left[:, 64:], right[:, 64:]], axis=1)


def weight_join(scalars, first, second):
    return pl.pallas_call(
        weight_join_kernel,
        grid_spec=pltpu.PrefetchScalarGridSpec(
            num_scalar_prefetch=1,
            grid=(1,),
            in_specs=[whole(4, 3, 128, 128)] * 2,
            out_specs=whole(128, 3072),
        ),
        out_shape=shape((128, 3072), jnp.float32),
        cost_estimate=pl.CostEstimate(flops=0, bytes_accessed=3 * 10**6, transcendentals=0),
        name="weight_join",
    )(scalars, first, second)


def spans(y):
    for s in range(4):
        for w in range(2):
            for t in range(4):
                xh, c = t // 2, t % 2
                start = 12 * lon_of(xh, lax.rem(y + s, 4), c) + 3 + 6 * w
                if xh == 1 and c == 1 and w == 1:
                    yield s, w, t, start, 0, 3
                    yield s, w, t, lax.rem(start + 3, 192), 3, 3
                else:
                    yield s, w, t, start, 0, 6


def token_split_kernel(s_ref, own_ref, rim_ref, out_ref, sems):
    copies = []
    for s, w, t, start, offset, columns in spans(s_ref[2]):
        for half, ref in enumerate((own_ref, rim_ref)):
            copies.append(pltpu.make_async_copy(
                ref.at[pl.ds(0, 6), pl.ds(start, columns)],
                out_ref.at[s, w, t, pl.ds(half * 6, 6), pl.ds(offset, columns)],
                sems.at[len(copies)]))
    for copy in copies:
        copy.start()
    for copy in copies:
        copy.wait()


def token_split(scalars, own, rim):
    return pl.pallas_call(
        token_split_kernel,
        grid_spec=pltpu.PrefetchScalarGridSpec(
            num_scalar_prefetch=1,
            grid=(1,),
            in_specs=[pl.BlockSpec(memory_space=pl.ANY)] * 2,
            out_specs=pl.BlockSpec(memory_space=pl.ANY),
            scratch_shapes=[pltpu.SemaphoreType.DMA((72,))],
        ),
        out_shape=shape((4, 2, 4, WLAT, WLON, LEVELS, 128)),
        cost_estimate=pl.CostEstimate(flops=0, bytes_accessed=3 * 10**6, transcendentals=0),
        name="token_split",
    )(scalars, own, rim)


def token_join_kernel(s_ref, *refs):
    near, far, out_ref, sems = refs[:8], refs[8:10], refs[10], refs[11]
    copies = []
    for s, w, t, start, offset, columns in spans(s_ref[2]):
        copies.append(pltpu.make_async_copy(
            near[w * 4 + s].at[t, pl.ds(0, 6), pl.ds(offset, columns)],
            out_ref.at[pl.ds(6, 6), pl.ds(start, columns)], sems.at[len(copies)]))
        copies.append(pltpu.make_async_copy(
            far[w].at[s, t, pl.ds(0, 6), pl.ds(offset, columns)],
            out_ref.at[pl.ds(0, 6), pl.ds(start, columns)], sems.at[len(copies)]))
    for copy in copies:
        copy.start()
    for copy in copies:
        copy.wait()


def token_join(scalars, near, far):
    return pl.pallas_call(
        token_join_kernel,
        grid_spec=pltpu.PrefetchScalarGridSpec(
            num_scalar_prefetch=1,
            grid=(1,),
            in_specs=[pl.BlockSpec(memory_space=pl.ANY)] * 10,
            out_specs=pl.BlockSpec(memory_space=pl.ANY),
            scratch_shapes=[pltpu.SemaphoreType.DMA((72,))],
        ),
        out_shape=shape((WLAT, 192, LEVELS, 128)),
        cost_estimate=pl.CostEstimate(flops=0, bytes_accessed=3 * 10**6, transcendentals=0),
        name="token_join",
    )(scalars, *near, *far)


def place_cotangent(i, c, us, ub):
    for step in range(2):
        @pl.when(i == step)
        def _():
            for dc in range(2):
                slot = pl.multiple_of((dc ^ c) * WTOK, WTOK)
                ub[pl.ds(slot, WTOK), :] = us[2 * step + dc][...]


def load_weights(ws, wfull, column, source):
    for s in range(4):
        for k in range(4):
            for part in range(3):
                wfull[(s * 4 + k) * 128:(s * 4 + k + 1) * 128, column + part * 128:column + (part + 1) * 128] = (
                    ws[s][source + k * 3 + part])


def load_out_rows(y, pair, ws, wout):
    for s in range(4):
        head = lax.rem(y + 4 - s, 4)

        @pl.when(lax.div(head, 2) == pair)
        def _():
            rows = pl.ds(pl.multiple_of(lax.rem(head, 2) * 64, 64), 64)
            for i in range(8):
                wout[rows, i * 256:i * 256 + 128] = ws[s][12 + i, 0:64]
                wout[rows, i * 256 + 128:i * 256 + 256] = ws[s][12 + i, 64:128]


def two_heads(nb, w_pair, cot, out_rows, split):
    qkv = mm(nb, w_pair, ((1,), (0,)))
    queries = (qkv[:, :128] * (HEAD_DIM ** -0.5)).astype(jnp.bfloat16)
    qkv = qkv.astype(jnp.bfloat16)
    grad_att = mm(cot, out_rows, ((1,), (1,))).astype(jnp.bfloat16)
    row_group = lax.broadcasted_iota(jnp.int32, (WTOK, WTOK), 0) >= HALF
    col_group = lax.broadcasted_iota(jnp.int32, (WTOK, WTOK), 1) >= HALF
    keep = (row_group == col_group) | (split == 0)
    att_rows, dqkv_rows = [], []
    for w in range(2):
        rows = slice(w * WTOK, (w + 1) * WTOK)
        att_h, dq_h, dk_h, dv_h = [], [], [], []
        for h in range(2):
            cols = slice(h * 64, (h + 1) * 64)
            q = queries[rows, cols]
            k = qkv[rows, 128:256][:, cols]
            v = qkv[rows, 256:384][:, cols]
            g = grad_att[rows, cols]
            scores = jnp.where(keep, mm(q, k, ((1,), (1,))), NEG_FILL)
            expons = jnp.exp(scores - jnp.max(scores, axis=-1, keepdims=True))
            attention = expons * (1.0 / jnp.sum(expons, axis=-1, keepdims=True))
            attention_b = attention.astype(jnp.bfloat16)
            att_h.append(mm(attention_b, v, ((1,), (0,))))
            weighted = attention * mm(g, v, ((1,), (1,)))
            inner = jnp.sum(weighted, axis=-1, keepdims=True)
            grad_scores = (weighted - attention * inner).astype(jnp.bfloat16)
            dq_h.append(mm(grad_scores, k, ((1,), (0,))) * (HEAD_DIM ** -0.5))
            dk_h.append(mm(grad_scores, q, ((0,), (0,))))
            dv_h.append(mm(attention_b, g, ((0,), (0,))))
        att_rows.append(jnp.concatenate(att_h, axis=1))
        dqkv_rows.append(jnp.concatenate(dq_h + dk_h + dv_h, axis=1))
    attended = jnp.concatenate(att_rows, axis=0).astype(jnp.bfloat16)
    dqkv = jnp.concatenate(dqkv_rows, axis=0).astype(jnp.bfloat16)
    return attended, dqkv


def first_kernel(add, s_ref, *refs):
    xs, us, ws = refs[:4], refs[4:8], refs[8:12]
    refs = refs[12:]
    prior = None
    if add:
        prior, refs = refs[0], refs[1:]
    nb_ref, inv_ref, dq_ref, gw_ref, wfull, wout, ub = refs
    i = pl.program_id(0)

    @pl.when(i == 0)
    def _():
        load_weights(ws, wfull, 0, 0)
        load_out_rows(s_ref[2], 0, ws, wout)
        gw_ref[...] = prior[...] if add else jnp.zeros_like(gw_ref)

    place_cotangent(i, s_ref[1], us, ub)
    x = jnp.concatenate(
        [xs[k][s].reshape(PAIR, 128) for s in range(4) for k in range(4)], axis=1
    ).astype(jnp.float32)
    centred = x - jnp.mean(x, axis=-1, keepdims=True)
    inverse = lax.rsqrt(jnp.mean(centred * centred, axis=-1, keepdims=True) + EPSILON)
    nb = (centred * inverse).astype(jnp.bfloat16)
    nb_ref[...] = nb
    inv_ref[...] = jnp.broadcast_to(inverse, inv_ref.shape)
    attended, dqkv = two_heads(nb, wfull[...], ub[...], wout[...], s_ref[3])
    dq_ref[...] = dqkv
    gw_ref[...] += mm(attended, ub[...], ((0,), (0,)))


def second_kernel(add, s_ref, *refs):
    nb_ref, inv_ref, before_ref = refs[:3]
    us, ws, vs = refs[3:7], refs[7:11], refs[11:15]
    refs = refs[15:]
    prior = None
    if add:
        prior, refs = refs[0], refs[1:]
    pc_ref, px_ref, po_ref, dq_ref, gw_ref, wfull, wout, ub = refs
    i = pl.program_id(0)
    y = s_ref[2]

    @pl.when(i == 0)
    def _():
        load_weights(ws, wfull, 0, 0)
        load_weights(vs, wfull, 384, 0)
        load_out_rows(y, 1, ws, wout)
        gw_ref[...] = prior[...] if add else jnp.zeros_like(gw_ref)

    place_cotangent(i, s_ref[1], us, ub)
    nb = nb_ref[...]
    attended, dqkv = two_heads(nb, wfull[:, 384:], ub[...], wout[...], s_ref[3])
    dq_ref[...] = dqkv
    gw_ref[...] += mm(attended, ub[...], ((0,), (0,)))
    grad_normal = mm(jnp.concatenate([before_ref[...], dqkv], axis=1), wfull[...], ((1,), (1,)))
    normal = nb.astype(jnp.float32)
    mean_one = jnp.mean(grad_normal, axis=-1, keepdims=True)
    mean_two = jnp.mean(grad_normal * normal, axis=-1, keepdims=True)
    grad_rolled = inv_ref[:, :1] * (grad_normal - mean_one - normal * mean_two)
    for s in range(4):
        part = [grad_rolled[:, (s * 4 + k) * 128:(s * 4 + k + 1) * 128].reshape(2, WTOK, 128) for k in range(4)]
        pc_ref[0, s] = part[1].astype(jnp.bfloat16)
        pc_ref[1, s] = part[3].astype(jnp.bfloat16)
        px_ref[s] = part[2].astype(jnp.bfloat16)
        block = lon_of(s_ref[0], lax.rem(y + 4 - s, 4), s_ref[1])
        own = ub[:, pl.ds(pl.multiple_of(block * 128, 128), 128)].astype(jnp.float32)
        po_ref[s] = part[0] + own.reshape(2, WTOK, 128)


WEIGHT_SCRATCH = [
    pltpu.VMEM((128, D), jnp.bfloat16),
    pltpu.VMEM((PAIR, D), jnp.bfloat16),
]


def first_pass(scalars, xs, us, ws, prior=None):
    more = [] if prior is None else [prior]
    return pl.pallas_call(
        functools.partial(first_kernel, prior is not None),
        grid_spec=pltpu.PrefetchScalarGridSpec(
            num_scalar_prefetch=1,
            grid=(2,),
            in_specs=[pl.BlockSpec((4, 2, WTOK, 128), lambda i, s: (0, i ^ s[0], 0, 0))] * 4
            + [whole(WTOK, D)] * 4 + [whole(20, 128, 128)] * 4 + [whole(128, D)] * len(more),
            out_specs=[
                pl.BlockSpec((PAIR, D), lambda i, s: (i, 0)),
                pl.BlockSpec((PAIR, 128), lambda i, s: (i, 0)),
                pl.BlockSpec((PAIR, 384), lambda i, s: (i, 0)),
                whole(128, D),
            ],
            scratch_shapes=[pltpu.VMEM((D, 384), jnp.bfloat16)] + WEIGHT_SCRATCH,
        ),
        out_shape=[
            shape((2 * PAIR, D)), shape((2 * PAIR, 128), jnp.float32), shape((2 * PAIR, 384)),
            shape((128, D), jnp.float32),
        ],
        compiler_params=pltpu.CompilerParams(vmem_limit_bytes=56 * MIB),
        cost_estimate=pl.CostEstimate(flops=8 * 10**9, bytes_accessed=12 * 10**6, transcendentals=10**6),
        name="heads_first",
    )(scalars, *xs, *us, *ws, *more)


def second_pass(scalars, nb, inverse, before, us, ws, vs, prior=None):
    more = [] if prior is None else [prior]
    tile = pl.BlockSpec((4, 2, WTOK, 128), lambda i, s: (0, i ^ s[0], 0, 0))
    return pl.pallas_call(
        functools.partial(second_kernel, prior is not None),
        grid_spec=pltpu.PrefetchScalarGridSpec(
            num_scalar_prefetch=1,
            grid=(2,),
            in_specs=[
                pl.BlockSpec((PAIR, D), lambda i, s: (i, 0)),
                pl.BlockSpec((PAIR, 128), lambda i, s: (i, 0)),
                pl.BlockSpec((PAIR, 384), lambda i, s: (i, 0)),
            ] + [whole(WTOK, D)] * 4 + [whole(20, 128, 128)] * 4 + [whole(12, 128, 128)] * 4
            + [whole(128, D)] * len(more),
            out_specs=[
                pl.BlockSpec((2, 4, 2, WTOK, 128), lambda i, s: (0, 0, i ^ s[0], 0, 0)),
                tile,
                tile,
                pl.BlockSpec((PAIR, 384), lambda i, s: (i, 0)),
                whole(128, D),
            ],
            scratch_shapes=[pltpu.VMEM((D, 768), jnp.bfloat16)] + WEIGHT_SCRATCH,
        ),
        out_shape=[
            shape((2, 4, 4, WTOK, 128)), shape((4, 4, WTOK, 128)), shape((4, 4, WTOK, 128), jnp.float32),
            shape((2 * PAIR, 384)), shape((128, D), jnp.float32),
        ],
        compiler_params=pltpu.CompilerParams(vmem_limit_bytes=56 * MIB),
        cost_estimate=pl.CostEstimate(flops=10 * 10**9, bytes_accessed=14 * 10**6, transcendentals=10**6),
        name="heads_second",
    )(scalars, nb, inverse, before, *us, *ws, *vs, *more)


def term_kernel(with_out, s_ref, *refs):
    nb0, nb1, dq0, dq1 = refs[:4]
    refs = refs[4:]
    if with_out:
        gws, refs = refs[:2], refs[2:]
    for s in range(4):
        cols = slice(s * 512, (s + 1) * 512)
        term = mm(nb0[:, cols], dq0[...], ((0,), (0,))) + mm(nb1[:, cols], dq1[...], ((0,), (0,)))
        out = refs[s]
        for k in range(4):
            for part in range(3):
                out[k * 3 + part] = term[k * 128:(k + 1) * 128, part * 128:(part + 1) * 128].astype(out.dtype)
        if with_out:
            head = lax.rem(s_ref[2] + 4 - s, 4)
            rows = pl.ds(pl.multiple_of(lax.rem(head, 2) * 64, 64), 64)
            for pair in range(2):
                @pl.when(lax.div(head, 2) == pair)
                def _():
                    for i in range(8):
                        out[12 + i, 0:64] = gws[pair][rows, i * 256:i * 256 + 128].astype(out.dtype)
                        out[12 + i, 64:128] = gws[pair][rows, i * 256 + 128:i * 256 + 256].astype(out.dtype)


def weight_terms(scalars, nbs, dqs, gws=()):
    blocks = 20 if gws else 12
    return pl.pallas_call(
        functools.partial(term_kernel, bool(gws)),
        grid_spec=pltpu.PrefetchScalarGridSpec(
            num_scalar_prefetch=1,
            grid=(1,),
            in_specs=[whole(2 * PAIR, D)] * 2 + [whole(2 * PAIR, 384)] * 2 + [whole(128, D)] * len(gws),
            out_specs=[whole(blocks, 128, 128)] * 4,
        ),
        out_shape=[shape((blocks, 128, 128), jnp.float32 if s == 0 else jnp.bfloat16) for s in range(4)],
        compiler_params=pltpu.CompilerParams(vmem_limit_bytes=40 * MIB),
        cost_estimate=pl.CostEstimate(flops=4 * 10**9, bytes_accessed=9 * 10**6, transcendentals=0),
        name="weight_terms",
    )(scalars, *nbs, *dqs, *gws)


def after(values, *earlier):
    return lax.optimization_barrier(tuple(values) + earlier)[:len(values)]


def local(tokens, upstream, qkv_weight, out_weight):
    half_lat = WLAT // 2
    half_lon = WLON // 2
    lon = lax.axis_index("lon")
    lat = lax.axis_index("lat")
    xh, y, c = lon // 8, (lon // 2) % 4, lon % 2
    last = (lat == lax.axis_size("lat") - 1).astype(jnp.int32)
    scalars = jnp.stack([xh, c, y, last]).astype(jnp.int32)

    rim = passed_along(tokens[:half_lat], "lat", -1)
    lat_rim = passed_along(upstream[:half_lat], "lat", -1)

    split, out_blocks = weight_split(scalars, qkv_weight, out_weight)
    from_c = swap_c(jnp.stack([split[1], split[3]]))
    from_x = swap_x(jnp.stack([split[2], from_c[1]]))
    rows = jnp.concatenate([jnp.stack([split[0], from_c[0]]), from_x])
    shard0 = jnp.concatenate([rows[:, :3].reshape(12, 128, 128), out_blocks])
    shard1 = rows[:, 3:].reshape(12, 128, 128)

    pieces = token_split(scalars, tokens[half_lat:], rim).reshape(4, 2, 4, WTOK, 128)
    got = [pieces[0]] + [shift_y(pieces[s], s) for s in (1, 2, 3)]
    x_own = [jnp.stack([got[s][w] for s in range(4)]) for w in range(2)]
    ws = [shard0] + [shift_y(shard0, s) for s in (1, 2, 3)]

    up = jnp.concatenate([upstream[half_lat:], lat_rim], axis=0)
    lon_rim = passed_along(up[:, :half_lon], "lon", -1)
    u_own = [
        up[:, half_lon:half_lon + WLON].reshape(WTOK, D),
        jnp.concatenate([up[:, half_lon + WLON:], lon_rim], axis=1).reshape(WTOK, D),
    ]

    x_c = [swap_c(x_own[0])]
    u_c = [swap_c(u_own[0])]
    x_x = [swap_x(x_own[0])]
    u_x = [swap_x(u_own[0])]
    x_own[1], u_own[1] = after((x_own[1], u_own[1]), x_x[0], u_x[0])
    x_x.append(swap_x(x_own[1]))
    u_x.append(swap_x(u_own[1]))
    x_c.append(swap_c(x_own[1]))
    u_c.append(swap_c(u_own[1]))
    xs = [[x_own[w], x_c[w], x_x[w], swap_c(x_x[w])] for w in range(2)]
    us = [[u_own[w], u_c[w], u_x[w], swap_c(u_x[w])] for w in range(2)]

    (shard1,) = after((shard1,), *ws[1:])
    vs = [shard1] + [shift_y(shard1, s) for s in (1, 2, 3)]

    nb0, inv0, dq00, gw0 = first_pass(scalars, xs[0], us[0], ws)
    part0 = second_pass(scalars, nb0, inv0, dq00, us[0], ws, vs)
    nb1, inv1, dq01, gw0 = first_pass(scalars, xs[1], us[1], ws, gw0)
    terms0 = weight_terms(scalars, (nb0, nb1), (dq00, dq01))
    part1 = second_pass(scalars, nb1, inv1, dq01, us[1], ws, vs, part0[4])
    terms1 = weight_terms(scalars, (nb0, nb1), (part0[3], part1[3]), (gw0, part1[4]))

    def summed(terms):
        return sum((shift_y(terms[s], -s).astype(jnp.float32) for s in (1, 3, 2)), terms[0])

    def gathered(total):
        blocks = total.reshape(4, 3, 128, 128)
        sent = blocks.astype(jnp.bfloat16)
        by_x = swap_x(sent[2:])
        by_c = swap_c(jnp.stack([sent[1], by_x[1]]))
        return jnp.stack([blocks[0]] + [v.astype(jnp.float32) for v in (by_c[0], by_x[0], by_c[1])])

    sum0 = summed(terms0)
    sum1 = summed(terms1)
    grad_qkv_w = weight_join(scalars, gathered(sum0), gathered(sum1[:12]))
    grad_out_w = sum1[12:].reshape(8, 2, 64, 128).transpose(2, 0, 1, 3).reshape(64, D)

    near, far = [], []
    for part_c, part_x, part_own in (part0[:3], part1[:3]):
        got_c = swap_c(part_c)
        got_x = swap_x((part_x.astype(jnp.float32) + got_c[1].astype(jnp.float32)).astype(jnp.bfloat16))
        full = (part_own + got_c[0].astype(jnp.float32) + got_x.astype(jnp.float32)).astype(jnp.bfloat16)
        back = [full[0]] + [shift_y(full[s], -s) for s in (1, 2, 3)]
        far.append(passed_along(jnp.stack([b[:, HALF:] for b in back]), "lat", 1))
        near += back
    near = [b.reshape(4, WLAT, WLON, LEVELS, 128) for b in near]
    far = [b.reshape(4, 4, WLAT // 2, WLON, LEVELS, 128) for b in far]
    result = token_join(scalars, near, far)
    return (result, grad_qkv_w[None], grad_out_w[None])


def solution(mesh):
    return jax.shard_map(
        local,
        mesh=mesh,
        in_specs=(
            P("lat", None, None, "lon"),
            P("lat", "lon", None, None),
            P("lon", None),
            P("lon", None),
        ),
        out_specs=(P("lat", None, None, "lon"), P("lat", "lon", None), P("lat", "lon", None)),
        check_vma=False,
    )
```

```python
import functools

import jax
import jax.numpy as jnp
from jax import lax
from jax.experimental import pallas as pl
from jax.experimental.pallas import tpu as pltpu
from jax.sharding import PartitionSpec as P

HEAD_DIM = 64
WLAT = 12
WLON = 6
LEVELS = 2
WTOK = WLAT * WLON * LEVELS
PAIR = 2 * WTOK
HALF = WTOK // 2
D = 2048
NY = 4
MIB = 1024 * 1024

NEG_FILL = -1e30
EPSILON = 1e-05


def lon_of(xh, y, c):
    return (xh * NY + y) * 2 + c


COORDS = [(xh, y, c) for xh in range(2) for y in range(NY) for c in range(2)]


ALONG_Y = [[lon_of(xh, y, c) for y in range(NY)] for xh in range(2) for c in range(2)]


def swap_c(value):
    return lax.ppermute(value, "lon", [(lon_of(x, y, c), lon_of(x, y, 1 - c)) for x, y, c in COORDS])


def swap_x(value):
    return lax.ppermute(value, "lon", [(lon_of(x, y, c), lon_of(1 - x, y, c)) for x, y, c in COORDS])


def shift_y(value, by):
    return lax.ppermute(value, "lon", [(lon_of(x, y, c), lon_of(x, (y + by) % NY, c)) for x, y, c in COORDS])


def moved(value, dlat, lon_map):
    rows, lons = lax.axis_size("lat"), lax.axis_size("lon")
    pairs = [
        (r * lons + i, (r + dlat) % rows * lons + lon_map(i)) for r in range(rows) for i in range(lons)
    ]
    return lax.ppermute(value, ("lat", "lon"), pairs)


def y_map(by):
    return lambda i: lon_of(i // 8, (i // 2 + by) % NY, i % 2)


def x_map(i):
    return lon_of(1 - i // 8, i // 2 % NY, i % 2)


def lon_map(by):
    return lambda i: (i + by) % 16


def mm(a, b, dims):
    return lax.dot_general(a, b, (dims, ((), ())), preferred_element_type=jnp.float32)


def shape(dims, dtype=jnp.bfloat16):
    return jax.ShapeDtypeStruct(dims, dtype)


def whole(*dims):
    return pl.BlockSpec(dims, lambda *_: (0,) * len(dims))


def weight_split_kernel(s_ref, q_ref, o_ref, w_ref, out_ref):
    group = s_ref[0] * 2 + s_ref[1]
    for xh in range(2):
        for c in range(2):
            slot = group ^ (xh * 2 + c)
            for part in range(3):
                for pair in range(2):
                    lo = (part * 8 + xh * 4 + pair * 2) * 128 + c * 64
                    w_ref[slot, part * 2 + pair] = jnp.concatenate(
                        [q_ref[:, lo:lo + 64], q_ref[:, lo + 128:lo + 192]], axis=1)
    for i in range(8):
        out_ref[i] = jnp.concatenate(
            [o_ref[:, i * 256:i * 256 + 128], o_ref[:, i * 256 + 128:i * 256 + 256]], axis=0)


def weight_split(scalars, qkv_weight, out_weight):
    return pl.pallas_call(
        weight_split_kernel,
        grid_spec=pltpu.PrefetchScalarGridSpec(
            num_scalar_prefetch=1,
            grid=(1,),
            in_specs=[whole(128, 3072), whole(64, D)],
            out_specs=[whole(4, 6, 128, 128), whole(8, 128, 128)],
        ),
        out_shape=[shape((4, 6, 128, 128)), shape((8, 128, 128))],
        cost_estimate=pl.CostEstimate(flops=0, bytes_accessed=2 * 10**6, transcendentals=0),
        name="weight_split",
    )(scalars, qkv_weight, out_weight)


def weight_join_kernel(s_ref, a_ref, b_ref, c_ref, out_ref):
    group = s_ref[0] * 2 + s_ref[1]

    def block(slot, index):
        return jnp.where(slot == 0, a_ref[index], jnp.where(
            slot == 1, b_ref[0, index].astype(jnp.float32), jnp.where(
                slot == 3, b_ref[1, index], c_ref[0, index]).astype(jnp.float32)))

    for xh in range(2):
        slots = [group ^ (xh * 2), group ^ (xh * 2 + 1)]
        for part in range(3):
            for pair in range(2):
                left, right = (block(slot, part * 2 + pair) for slot in slots)
                lo = (part * 8 + xh * 4 + pair * 2) * 128
                out_ref[:, lo:lo + 128] = jnp.concatenate([left[:, :64], right[:, :64]], axis=1)
                out_ref[:, lo + 128:lo + 256] = jnp.concatenate([left[:, 64:], right[:, 64:]], axis=1)


def weight_join(scalars, own, by_c, by_x):
    return pl.pallas_call(
        weight_join_kernel,
        grid_spec=pltpu.PrefetchScalarGridSpec(
            num_scalar_prefetch=1,
            grid=(1,),
            in_specs=[whole(6, 128, 128), whole(2, 6, 128, 128), whole(2, 6, 128, 128)],
            out_specs=whole(128, 3072),
        ),
        out_shape=shape((128, 3072), jnp.float32),
        cost_estimate=pl.CostEstimate(flops=0, bytes_accessed=3 * 10**6, transcendentals=0),
        name="weight_join",
    )(scalars, own, by_c, by_x)


def spans(y):
    for s in range(4):
        for w in range(2):
            for t in range(4):
                xh, c = t // 2, t % 2
                start = 12 * lon_of(xh, lax.rem(y + s, 4), c) + 3 + 6 * w
                if xh == 1 and c == 1 and w == 1:
                    yield s, w, t, start, 0, 3
                    yield s, w, t, lax.rem(start + 3, 192), 3, 3
                else:
                    yield s, w, t, start, 0, 6


def token_split_kernel(s_ref, tok_ref, *outs):
    for s, w, t, start, offset, columns in spans(s_ref[2]):
        for half in range(2):
            outs[s][half, w, t, :, offset:offset + columns] = (
                tok_ref[6 - half * 6:12 - half * 6, pl.ds(start, columns)])


def token_split(scalars, tokens):
    dims = (2, 2, 4, 6, WLON, LEVELS, 128)
    return pl.pallas_call(
        token_split_kernel,
        grid_spec=pltpu.PrefetchScalarGridSpec(
            num_scalar_prefetch=1,
            grid=(1,),
            in_specs=[whole(WLAT, 192, LEVELS, 128)],
            out_specs=[whole(*dims)] * 4,
        ),
        out_shape=[shape(dims)] * 4,
        compiler_params=pltpu.CompilerParams(vmem_limit_bytes=40 * MIB),
        cost_estimate=pl.CostEstimate(flops=0, bytes_accessed=3 * 10**6, transcendentals=0),
        name="token_split",
    )(scalars, tokens)


def token_join_kernel(s_ref, *refs):
    parts, out_ref = refs[:4], refs[4]
    for s, w, t, start, offset, columns in spans(s_ref[2]):
        out_ref[6:12, pl.ds(start, columns)] = parts[s][w, t, 0:6, offset:offset + columns]
        out_ref[0:6, pl.ds(start, columns)] = parts[s][w, t, 6:12, offset:offset + columns]


def token_join(scalars, parts):
    return pl.pallas_call(
        token_join_kernel,
        grid_spec=pltpu.PrefetchScalarGridSpec(
            num_scalar_prefetch=1,
            grid=(1,),
            in_specs=[whole(2, 4, WLAT, WLON, LEVELS, 128)] * 4,
            out_specs=whole(WLAT, 192, LEVELS, 128),
        ),
        out_shape=shape((WLAT, 192, LEVELS, 128)),
        compiler_params=pltpu.CompilerParams(vmem_limit_bytes=40 * MIB),
        cost_estimate=pl.CostEstimate(flops=0, bytes_accessed=3 * 10**6, transcendentals=0),
        name="token_join",
    )(scalars, *parts)


def attend(qkv, grad_att, split):
    scale = HEAD_DIM ** -0.5
    lane = lax.broadcasted_iota(jnp.int32, (1, 128), 1)
    row_group = lax.broadcasted_iota(jnp.int32, (WTOK, WTOK), 0) >= HALF
    col_group = lax.broadcasted_iota(jnp.int32, (WTOK, WTOK), 1) >= HALF
    keep = (row_group == col_group) | (split == 0)
    units = []
    for w in range(2):
        rows = slice(w * WTOK, (w + 1) * WTOK)
        for pair in range(2):
            cols = slice(pair * 128, (pair + 1) * 128)
            q = qkv[rows, 0:256][:, cols] * scale
            k = qkv[rows, 256:512][:, cols]
            v = qkv[rows, 512:768][:, cols]
            g = grad_att[rows, cols]
            heads = []
            for h in range(2):
                mine = (lane < 64) == (h == 0)
                heads.append((
                    jnp.where(mine, q, 0.0).astype(jnp.bfloat16),
                    jnp.where(mine, g, 0.0).astype(jnp.bfloat16),
                ))
            kb, vb = k.astype(jnp.bfloat16), v.astype(jnp.bfloat16)
            units.append((heads, kb, vb, k.T.astype(jnp.bfloat16), v.T.astype(jnp.bfloat16)))
    work = [(u, h) for u in range(4) for h in range(2)]
    scores = {
        (u, h): mm(units[u][1], units[u][0][h][0], ((1,), (1,))) for u, h in work
    }
    probs, probs_b = {}, {}
    for key in work:
        kept = jnp.where(keep, scores[key], NEG_FILL)
        expons = jnp.exp(kept - jnp.max(kept, axis=0, keepdims=True))
        probs[key] = expons * (1.0 / jnp.sum(expons, axis=0, keepdims=True))
        probs_b[key] = probs[key].astype(jnp.bfloat16)
    grads = {}
    for u, h in work:
        weighted = probs[u, h] * mm(units[u][2], units[u][0][h][1], ((1,), (1,)))
        inner = jnp.sum(weighted, axis=0, keepdims=True)
        grads[u, h] = (weighted - probs[u, h] * inner).astype(jnp.bfloat16)
    att, dq, dk, dv = [], [], [], []
    for u in range(4):
        heads, _, _, kt, vt = units[u]
        att.append(jnp.concatenate(
            [mm(vt[h * 64:(h + 1) * 64], probs_b[u, h], ((1,), (0,))) for h in range(2)], axis=0).T)
        dq.append(jnp.concatenate(
            [mm(kt[h * 64:(h + 1) * 64], grads[u, h], ((1,), (0,))) for h in range(2)], axis=0).T * scale)
        dk.append(sum(mm(grads[u, h], heads[h][0], ((1,), (0,))) for h in range(2)))
        dv.append(sum(mm(probs_b[u, h], heads[h][1], ((1,), (0,))) for h in range(2)))
    attended = jnp.concatenate([jnp.concatenate(att[2 * w:2 * w + 2], axis=1) for w in range(2)], axis=0)
    dqkv = jnp.concatenate([
        jnp.concatenate(dq[2 * w:2 * w + 2] + dk[2 * w:2 * w + 2] + dv[2 * w:2 * w + 2], axis=1)
        for w in range(2)], axis=0)
    return attended.astype(jnp.bfloat16), dqkv.astype(jnp.bfloat16)


def window_kernel(s_ref, *refs):
    xs, us, w_ref = refs[:4], refs[4:8], refs[8]
    pc_ref, px_ref, po_ref, term_ref = refs[9:13]
    wfull, wout, ub, gacc, nb_all, dq_all = refs[13:]
    i = pl.program_id(0)
    c, y = s_ref[1], s_ref[2]

    @pl.when(i == 0)
    def _():
        for s in range(4):
            head = lax.rem(y + 4 - s, 4)

            def block(index):
                return w_ref[head * 32 + index]

            for k in range(4):
                row = (s * 4 + k) * 128
                for part in range(6):
                    wfull[row:row + 128, part * 128:(part + 1) * 128] = block(k * 6 + part)
            rows = pl.ds(pl.multiple_of(head * 64, 64), 64)
            for j in range(8):
                wout[rows, j * 256:j * 256 + 128] = block(24 + j)[0:64]
                wout[rows, j * 256 + 128:j * 256 + 256] = block(24 + j)[64:128]
        gacc[...] = jnp.zeros_like(gacc)

    for step in range(4):
        @pl.when(i == step)
        def _():
            for dc in range(2):
                ub[pl.ds(pl.multiple_of((dc ^ c) * WTOK, WTOK), WTOK), :] = us[2 * (step % 2) + dc][0]

    x = jnp.concatenate(
        [xs[k][s, 0].reshape(PAIR, 128) for s in range(4) for k in range(4)], axis=1
    ).astype(jnp.float32)
    centred = x - jnp.mean(x, axis=-1, keepdims=True)
    inverse = lax.rsqrt(jnp.mean(centred * centred, axis=-1, keepdims=True) + EPSILON)
    nb = (centred * inverse).astype(jnp.bfloat16)
    rows = pl.ds(pl.multiple_of(i * PAIR, PAIR), PAIR)
    nb_all[rows, :] = nb
    qkv = mm(nb, wfull[...], ((1,), (0,)))
    grad_att = mm(ub[...], wout[...], ((1,), (1,)))
    attended, dqkv = attend(qkv, grad_att, s_ref[3])
    dq_all[rows, :] = dqkv
    gacc[...] += mm(attended, ub[...], ((0,), (0,)))
    grad_normal = mm(dqkv, wfull[...], ((1,), (1,)))
    normal = nb_all[rows, :].astype(jnp.float32)
    mean_one = jnp.mean(grad_normal, axis=-1, keepdims=True)
    mean_two = jnp.mean(grad_normal * normal, axis=-1, keepdims=True)
    grad_rolled = inverse * (grad_normal - mean_one - normal * mean_two)

    for s in range(4):
        part = [grad_rolled[:, (s * 4 + k) * 128:(s * 4 + k + 1) * 128].reshape(2, WTOK, 128) for k in range(4)]
        pc_ref[0, s, 0] = part[1].astype(jnp.bfloat16)
        pc_ref[1, s, 0] = part[3].astype(jnp.bfloat16)
        px_ref[s, 0] = part[2].astype(jnp.bfloat16)
        block = lon_of(s_ref[0], lax.rem(y + 4 - s, 4), c)
        own = ub[:, pl.ds(pl.multiple_of(block * 128, 128), 128)].astype(jnp.float32)
        po_ref[s, 0] = part[0] + own.reshape(2, WTOK, 128)

    @pl.when(i == 3)
    def _():
        for s in range(4):
            head = lax.rem(y + 4 - s, 4)
            term = mm(nb_all[:, s * 512:(s + 1) * 512], dq_all[...], ((0,), (0,))).astype(jnp.bfloat16)
            for k in range(4):
                for part in range(6):
                    term_ref[head * 32 + k * 6 + part] = term[k * 128:(k + 1) * 128, part * 128:(part + 1) * 128]
            gw = gacc[pl.ds(pl.multiple_of(head * 64, 64), 64), :].astype(jnp.bfloat16)
            for j in range(8):
                term_ref[head * 32 + 24 + j] = jnp.concatenate(
                    [gw[:, j * 256:j * 256 + 128], gw[:, j * 256 + 128:j * 256 + 256]], axis=0)


def once(*dims):
    return pl.BlockSpec(dims, lambda *_: (0,) * len(dims), pipeline_mode=pl.Buffered(1))


def window_pass(scalars, xs, us, weights):
    tile = pl.BlockSpec((4, 1, 2, WTOK, 128), lambda i, s: (0, i // 2, (i % 2) ^ s[0], 0, 0))
    part_specs = [
        pl.BlockSpec((2, 4, 1, 2, WTOK, 128), lambda i, s: (0, 0, i // 2, (i % 2) ^ s[0], 0, 0)), tile, tile,
    ]
    part_shapes = [
        shape((2, 4, 2, 4, WTOK, 128)), shape((4, 2, 4, WTOK, 128)), shape((4, 2, 4, WTOK, 128), jnp.float32),
    ]
    return pl.pallas_call(
        window_kernel,
        grid_spec=pltpu.PrefetchScalarGridSpec(
            num_scalar_prefetch=1,
            grid=(4,),
            in_specs=[tile] * 4 + [pl.BlockSpec((1, WTOK, D), lambda i, s: (i // 2, 0, 0))] * 4
            + [once(128, 128, 128)],
            out_specs=part_specs + [once(128, 128, 128)],
            scratch_shapes=[
                pltpu.VMEM((D, 768), jnp.bfloat16),
                pltpu.VMEM((256, D), jnp.bfloat16),
                pltpu.VMEM((PAIR, D), jnp.bfloat16),
                pltpu.VMEM((256, D), jnp.float32),
                pltpu.VMEM((4 * PAIR, D), jnp.bfloat16),
                pltpu.VMEM((4 * PAIR, 768), jnp.bfloat16),
            ],
        ),
        out_shape=part_shapes + [shape((128, 128, 128))],
        compiler_params=pltpu.CompilerParams(vmem_limit_bytes=60 * MIB),
        cost_estimate=pl.CostEstimate(flops=32 * 10**9, bytes_accessed=30 * 10**6, transcendentals=10**6),
        name="window_pass",
    )(scalars, *xs, *us, weights)


def after(values, *earlier):
    return lax.optimization_barrier(tuple(values) + earlier)[:len(values)]


def local(tokens, upstream, qkv_weight, out_weight):
    lon = lax.axis_index("lon")
    lat = lax.axis_index("lat")
    xh, y, c = lon // 8, (lon // 2) % 4, lon % 2
    last = (lat == lax.axis_size("lat") - 1).astype(jnp.int32)
    scalars = jnp.stack([jnp.int32(v) for v in (xh, c, y, last)])

    split, out_blocks = weight_split(scalars, qkv_weight, out_weight)
    from_c = swap_c(jnp.stack([split[1], split[3]]))
    from_x = swap_x(jnp.stack([split[2], from_c[1]]))

    stay = lon_map(0)
    next_cols = moved(upstream[:, :3], 0, lon_map(-1))
    cols = jnp.concatenate([upstream[:, 3:], next_cols], axis=1)
    cols = cols.reshape(2, 6, 2, WLON, LEVELS, D).transpose(0, 2, 1, 3, 4, 5)
    u_low, u_high = cols[0], cols[1]
    u_low, u_high = after((u_low, u_high), from_x)
    u_x = [swap_x(u_high), moved(u_low, -1, x_map)]
    u_own = [u_high, moved(u_low, -1, stay)]
    u_own, u_x = (jnp.concatenate(u, axis=1).reshape(2, WTOK, D) for u in (u_own, u_x))
    us = [u_own, swap_c(u_own), u_x, swap_c(u_x)]

    pieces = token_split(scalars, tokens)
    pieces = [pieces[0]] + [shift_y(pieces[s], s) for s in (1, 2, 3)]
    x_high = jnp.stack([piece[0] for piece in pieces])
    x_low = jnp.stack([piece[1] for piece in pieces])
    x_x = [swap_x(x_high), moved(x_low, -1, x_map)]
    x_own = [x_high, moved(x_low, -1, stay)]
    x_own, x_x = (jnp.concatenate(v, axis=3).reshape(4, 2, 4, WTOK, 128) for v in (x_own, x_x))

    shard = jnp.concatenate(
        [split[0], from_c[0], from_x.reshape(12, 128, 128), out_blocks])
    (shard,) = after((shard,), next_cols, *pieces[1:])
    weights = lax.all_gather(shard, "lon", axis=0, tiled=True, axis_index_groups=ALONG_Y)
    xs = [x_own, swap_c(x_own), x_x, swap_c(x_x)]

    part_c, part_x, part_own, terms = window_pass(scalars, xs, us, weights)

    got_c = swap_c(part_c)
    own = part_own + got_c[0].astype(jnp.float32)
    other = (part_x.astype(jnp.float32) + got_c[1].astype(jnp.float32)).astype(jnp.bfloat16)
    own_low = own[..., HALF:, :].astype(jnp.bfloat16)

    high = own[..., :HALF, :] + swap_x(other[..., :HALF, :]).astype(jnp.float32)
    low = moved(own_low, 1, stay).astype(jnp.float32) + moved(other[..., HALF:, :], 1, x_map).astype(jnp.float32)
    full = jnp.concatenate([high, low], axis=3).astype(jnp.bfloat16)
    back = [full[0]] + [shift_y(full[s], -s) for s in (1, 2, 3)]

    total = lax.psum_scatter(
        terms, "lon", scatter_dimension=0, tiled=True, axis_index_groups=ALONG_Y).astype(jnp.float32)
    (total,) = after((total,), full)
    blocks = total[:24].reshape(4, 6, 128, 128)
    sent = blocks.astype(jnp.bfloat16)
    by_x = swap_x(sent[2:])
    (near_x,) = after((by_x,), *back)
    by_c = swap_c(jnp.stack([sent[1], near_x[1]]))
    grad_qkv_w = weight_join(scalars, blocks[0], by_c, by_x)
    grad_out_w = total[24:].reshape(8, 2, 64, 128).transpose(2, 0, 1, 3).reshape(64, D)

    result = token_join(scalars, [b.reshape(2, 4, WLAT, WLON, LEVELS, 128) for b in back])
    return (result, grad_qkv_w[None], grad_out_w[None])


def solution(mesh):
    return jax.shard_map(
        local,
        mesh=mesh,
        in_specs=(
            P("lat", None, None, "lon"),
            P("lat", "lon", None, None),
            P("lon", None),
            P("lon", None),
        ),
        out_specs=(P("lat", None, None, "lon"), P("lat", "lon", None), P("lat", "lon", None)),
        check_vma=False,
    )
```

```python
import functools

import jax
import jax.numpy as jnp
from jax import lax
from jax.experimental import pallas as pl
from jax.experimental.pallas import tpu as pltpu
from jax.sharding import PartitionSpec as P

HEAD_DIM = 64
WLAT = 12
WLON = 6
LEVELS = 2
WTOK = WLAT * WLON * LEVELS
PAIR = 2 * WTOK
HALF = WTOK // 2
D = 2048
NY = 4
MIB = 1024 * 1024

NEG_FILL = -1e30
EPSILON = 1e-05


def lon_of(xh, y, c):
    return (xh * NY + y) * 2 + c


COORDS = [(xh, y, c) for xh in range(2) for y in range(NY) for c in range(2)]


def swap_c(value):
    return lax.ppermute(value, "lon", [(lon_of(x, y, c), lon_of(x, y, 1 - c)) for x, y, c in COORDS])


def swap_x(value):
    return lax.ppermute(value, "lon", [(lon_of(x, y, c), lon_of(1 - x, y, c)) for x, y, c in COORDS])


def shift_y(value, by):
    return lax.ppermute(value, "lon", [(lon_of(x, y, c), lon_of(x, (y + by) % NY, c)) for x, y, c in COORDS])


def hop_z(value, by):
    rows, lons = lax.axis_size("lat"), lax.axis_size("lon")
    pairs = [
        (r * lons + i, (r + (2 * by if r % 2 == 0 else 0)) % rows * lons + i) for r in range(rows) for i in range(lons)
    ]
    return lax.ppermute(value, ("lat", "lon"), pairs)


def across(value, other):
    rows, lons = lax.axis_size("lat"), lax.axis_size("lon")
    pairs = [
        (r * lons + i, (r ^ 1) * lons + (lon_of(1 - i // 8, i // 2 % NY, i % 2) if other else i))
        for r in range(rows) for i in range(lons)
    ]
    return lax.ppermute(value, ("lat", "lon"), pairs)


def next_lon(value):
    return lax.ppermute(value, "lon", [(i, (i - 1) % 16) for i in range(16)])


def mm(a, b, dims):
    return lax.dot_general(a, b, (dims, ((), ())), preferred_element_type=jnp.float32)


def shape(dims, dtype=jnp.bfloat16):
    return jax.ShapeDtypeStruct(dims, dtype)


def whole(*dims):
    return pl.BlockSpec(dims, lambda *_: (0,) * len(dims))


def weight_split_kernel(s_ref, q_ref, o_ref, w_ref, out_ref):
    group = s_ref[0] * 2 + s_ref[1]
    for xh in range(2):
        for c in range(2):
            slot = group ^ (xh * 2 + c)
            for part in range(3):
                for pair in range(2):
                    lo = (part * 8 + xh * 4 + pair * 2) * 128 + c * 64
                    w_ref[slot, part * 2 + pair] = jnp.concatenate(
                        [q_ref[:, lo:lo + 64], q_ref[:, lo + 128:lo + 192]], axis=1)
    for i in range(8):
        out_ref[i] = jnp.concatenate(
            [o_ref[:, i * 256:i * 256 + 128], o_ref[:, i * 256 + 128:i * 256 + 256]], axis=0)


def weight_split(scalars, qkv_weight, out_weight):
    return pl.pallas_call(
        weight_split_kernel,
        grid_spec=pltpu.PrefetchScalarGridSpec(
            num_scalar_prefetch=1,
            grid=(1,),
            in_specs=[whole(128, 3072), whole(64, D)],
            out_specs=[whole(4, 6, 128, 128), whole(8, 128, 128)],
        ),
        out_shape=[shape((4, 6, 128, 128)), shape((8, 128, 128))],
        cost_estimate=pl.CostEstimate(flops=0, bytes_accessed=2 * 10**6, transcendentals=0),
        name="weight_split",
    )(scalars, qkv_weight, out_weight)


def weight_join_kernel(s_ref, a_ref, b_ref, c_ref, out_ref):
    group = s_ref[0] * 2 + s_ref[1]

    def block(slot, index):
        return jnp.where(slot == 0, a_ref[index], jnp.where(
            slot == 1, b_ref[0, index].astype(jnp.float32), jnp.where(
                slot == 3, b_ref[1, index], c_ref[0, index]).astype(jnp.float32)))

    for xh in range(2):
        slots = [group ^ (xh * 2), group ^ (xh * 2 + 1)]
        for part in range(3):
            for pair in range(2):
                left, right = (block(slot, part * 2 + pair) for slot in slots)
                lo = (part * 8 + xh * 4 + pair * 2) * 128
                out_ref[:, lo:lo + 128] = jnp.concatenate([left[:, :64], right[:, :64]], axis=1)
                out_ref[:, lo + 128:lo + 256] = jnp.concatenate([left[:, 64:], right[:, 64:]], axis=1)


def weight_join(scalars, own, by_c, by_x):
    return pl.pallas_call(
        weight_join_kernel,
        grid_spec=pltpu.PrefetchScalarGridSpec(
            num_scalar_prefetch=1,
            grid=(1,),
            in_specs=[whole(6, 128, 128), whole(2, 6, 128, 128), whole(2, 6, 128, 128)],
            out_specs=whole(128, 3072),
        ),
        out_shape=shape((128, 3072), jnp.float32),
        compiler_params=pltpu.CompilerParams(vmem_limit_bytes=60 * MIB),
        cost_estimate=pl.CostEstimate(flops=0, bytes_accessed=3 * 10**6, transcendentals=0),
        name="weight_join",
    )(scalars, own, by_c, by_x)


def spans(y):
    for s in range(4):
        for w in range(2):
            for t in range(4):
                xh, c = t // 2, t % 2
                start = 12 * lon_of(xh, lax.rem(y + s, 4), c) + 3 + 6 * w
                if xh == 1 and c == 1 and w == 1:
                    yield s, w, t, start, 0, 3
                    yield s, w, t, lax.rem(start + 3, 192), 3, 3
                else:
                    yield s, w, t, start, 0, 6


def token_split_kernel(s_ref, high_ref, low_ref, *outs):
    for s, w, t, start, offset, columns in spans(s_ref[2]):
        for half, ref in enumerate((high_ref, low_ref)):
            outs[s][half, w, t, :, offset:offset + columns] = ref[:, pl.ds(start, columns)]


def token_split(scalars, tokens, low):
    dims = (2, 2, 4, 6, WLON, LEVELS, 128)
    return pl.pallas_call(
        token_split_kernel,
        grid_spec=pltpu.PrefetchScalarGridSpec(
            num_scalar_prefetch=1,
            grid=(1,),
            in_specs=[
                pl.BlockSpec((6, 192, LEVELS, 128), lambda i, r: (1, 0, 0, 0)), whole(6, 192, LEVELS, 128),
            ],
            out_specs=[whole(*dims)] * 4,
        ),
        out_shape=[shape(dims)] * 4,
        compiler_params=pltpu.CompilerParams(vmem_limit_bytes=40 * MIB),
        cost_estimate=pl.CostEstimate(flops=0, bytes_accessed=3 * 10**6, transcendentals=0),
        name="token_split",
    )(scalars, tokens, low)


def token_join_kernel(s_ref, *refs):
    parts, out_ref = refs[:4], refs[4]
    for s, w, t, start, offset, columns in spans(s_ref[2]):
        out_ref[6:12, pl.ds(start, columns)] = parts[s][w, t, 0:6, offset:offset + columns]
        out_ref[0:6, pl.ds(start, columns)] = parts[s][w, t, 6:12, offset:offset + columns]


def token_join(scalars, parts):
    return pl.pallas_call(
        token_join_kernel,
        grid_spec=pltpu.PrefetchScalarGridSpec(
            num_scalar_prefetch=1,
            grid=(1,),
            in_specs=[whole(2, 4, WLAT, WLON, LEVELS, 128)] * 4,
            out_specs=whole(WLAT, 192, LEVELS, 128),
        ),
        out_shape=shape((WLAT, 192, LEVELS, 128)),
        compiler_params=pltpu.CompilerParams(vmem_limit_bytes=40 * MIB),
        cost_estimate=pl.CostEstimate(flops=0, bytes_accessed=3 * 10**6, transcendentals=0),
        name="token_join",
    )(scalars, *parts)


def attend(qkv, grad_att, split):
    scale = HEAD_DIM ** -0.5
    lane = lax.broadcasted_iota(jnp.int32, (1, 128), 1)
    row_group = lax.broadcasted_iota(jnp.int32, (WTOK, WTOK), 0) >= HALF
    col_group = lax.broadcasted_iota(jnp.int32, (WTOK, WTOK), 1) >= HALF
    keep = (row_group == col_group) | (split == 0)
    units = []
    for w in range(2):
        rows = slice(w * WTOK, (w + 1) * WTOK)
        for pair in range(2):
            cols = slice(pair * 128, (pair + 1) * 128)
            q = qkv[rows, 0:256][:, cols] * scale
            k = qkv[rows, 256:512][:, cols]
            v = qkv[rows, 512:768][:, cols]
            g = grad_att[rows, cols]
            heads = []
            for h in range(2):
                mine = (lane < 64) == (h == 0)
                heads.append((
                    jnp.where(mine, q, 0.0).astype(jnp.bfloat16),
                    jnp.where(mine, g, 0.0).astype(jnp.bfloat16),
                ))
            kb, vb = k.astype(jnp.bfloat16), v.astype(jnp.bfloat16)
            units.append((heads, kb, vb, k.T.astype(jnp.bfloat16), v.T.astype(jnp.bfloat16)))
    work = [(u, h) for u in range(4) for h in range(2)]
    scores = {
        (u, h): mm(units[u][1], units[u][0][h][0], ((1,), (1,))) for u, h in work
    }
    probs, probs_b = {}, {}
    for key in work:
        kept = jnp.where(keep, scores[key], NEG_FILL)
        expons = jnp.exp(kept - jnp.max(kept, axis=0, keepdims=True))
        probs[key] = expons * (1.0 / jnp.sum(expons, axis=0, keepdims=True))
        probs_b[key] = probs[key].astype(jnp.bfloat16)
    grads = {}
    for u, h in work:
        weighted = probs[u, h] * mm(units[u][2], units[u][0][h][1], ((1,), (1,)))
        inner = jnp.sum(weighted, axis=0, keepdims=True)
        grads[u, h] = (weighted - probs[u, h] * inner).astype(jnp.bfloat16)
    att, dq, dk, dv = [], [], [], []
    for u in range(4):
        heads, _, _, kt, vt = units[u]
        att.append(jnp.concatenate(
            [mm(vt[h * 64:(h + 1) * 64], probs_b[u, h], ((1,), (0,))) for h in range(2)], axis=0).T)
        dq.append(jnp.concatenate(
            [mm(kt[h * 64:(h + 1) * 64], grads[u, h], ((1,), (0,))) for h in range(2)], axis=0).T * scale)
        dk.append(sum(mm(grads[u, h], heads[h][0], ((1,), (0,))) for h in range(2)))
        dv.append(sum(mm(probs_b[u, h], heads[h][1], ((1,), (0,))) for h in range(2)))
    attended = jnp.concatenate([jnp.concatenate(att[2 * w:2 * w + 2], axis=1) for w in range(2)], axis=0)
    dqkv = jnp.concatenate([
        jnp.concatenate(dq[2 * w:2 * w + 2] + dk[2 * w:2 * w + 2] + dv[2 * w:2 * w + 2], axis=1)
        for w in range(2)], axis=0)
    return attended.astype(jnp.bfloat16), dqkv.astype(jnp.bfloat16)


ORDER = (2, 1, 3, 0)


def window_kernel(s_ref, *refs):
    highs, lows, us, ws = refs[:4], refs[4:8], refs[8:12], refs[12:17]
    pc_ref, px_ref, po_ref = refs[17:20]
    terms = refs[20:25]
    wfull, wout, ub, gacc, nb_all, dq_all, wsum, att_all = refs[25:]
    i = pl.program_id(0)
    c, y = s_ref[1], s_ref[2]

    @pl.when(i == 0)
    def _():
        for s in range(4):
            def block(index):
                if s == 2:
                    return ws[2][index] if index < 16 else ws[4][index - 16]
                return ws[s][index]
            for k in range(4):
                row = (s * 4 + k) * 128
                for part in range(6):
                    wfull[row:row + 128, part * 128:(part + 1) * 128] = block((0, 2, 1, 3)[k] * 6 + part)
            head = lax.rem(y + 4 - s, 4)
            rows = pl.ds(pl.multiple_of(head * 64, 64), 64)
            for j in range(8):
                wout[rows, j * 256:j * 256 + 128] = block(24 + j)[0:64]
                wout[rows, j * 256 + 128:j * 256 + 256] = block(24 + j)[64:128]
        wsum[...] = jnp.sum(wfull[...].astype(jnp.float32), axis=0, keepdims=True)

    rows = pl.ds(pl.multiple_of(i * PAIR, PAIR), PAIR)
    for step in range(4):
        @pl.when(i == step)
        def _():
            for dc in range(2):
                ub[pl.ds(pl.multiple_of(step * PAIR + (dc ^ c) * WTOK, WTOK), WTOK), :] = us[2 * (step % 2) + dc][0]

    x = jnp.concatenate([
        jnp.concatenate(
            [half[k][s, 0].astype(jnp.float32) for half in (highs, lows)], axis=1).reshape(PAIR, 128)
        for s in range(4) for k in range(4)
    ], axis=1)
    centred = x - jnp.mean(x, axis=-1, keepdims=True)
    inverse = lax.rsqrt(jnp.mean(centred * centred, axis=-1, keepdims=True) + EPSILON)
    nb = (centred * inverse).astype(jnp.bfloat16)
    nb_all[rows, :] = nb
    qkv = mm(nb, wfull[...], ((1,), (0,)))
    grad_att = mm(ub[rows, :], wout[...], ((1,), (1,)))
    attended, dqkv = attend(qkv, grad_att, s_ref[3])
    att_all[rows, :] = attended
    dq_all[rows, :] = dqkv
    dqkv_f = dqkv.astype(jnp.float32)
    mean_one = jnp.sum(dqkv_f * wsum[...], axis=-1, keepdims=True) * (inverse / D)
    mean_two = jnp.sum(dqkv_f * qkv, axis=-1, keepdims=True) * (inverse / D)
    grad_normal = mm(dqkv, wfull[...], ((1,), (1,)))
    normal = nb_all[rows, :].astype(jnp.float32)
    grad_rolled = inverse * grad_normal - mean_one - normal * mean_two

    for s in range(4):
        part = [grad_rolled[:, (s * 4 + k) * 128:(s * 4 + k + 1) * 128].reshape(2, WTOK, 128) for k in range(4)]
        pc_ref[0, s, 0] = part[1].astype(jnp.bfloat16)
        pc_ref[1, s, 0] = part[3].astype(jnp.bfloat16)
        px_ref[s, 0] = part[2].astype(jnp.bfloat16)
        block = lon_of(s_ref[0], lax.rem(y + 4 - s, 4), c)
        own = ub[rows, pl.ds(pl.multiple_of(block * 128, 128), 128)].astype(jnp.float32)
        po_ref[s, 0] = part[0] + own.reshape(2, WTOK, 128)

    @pl.when(i == 3)
    def _():
        gacc[...] = mm(att_all[...], ub[...], ((0,), (0,)))
        for step, s in enumerate(ORDER):
            mine = terms[:2] if s == 2 else terms[step + 1:step + 2]
            size = mine[0].shape[0]

            def put(index, value):
                out = mine[index // size]
                out[index % size] = value.astype(out.dtype)

            term = mm(nb_all[:, s * 512:(s + 1) * 512], dq_all[...], ((0,), (0,)))
            for k in range(4):
                for part in range(6):
                    put(k * 6 + part, term[k * 128:(k + 1) * 128, part * 128:(part + 1) * 128])
            head = lax.rem(y + 4 - s, 4)
            gw = gacc[pl.ds(pl.multiple_of(head * 64, 64), 64), :]
            for j in range(8):
                put(24 + j, jnp.concatenate(
                    [gw[:, j * 256:j * 256 + 128], gw[:, j * 256 + 128:j * 256 + 256]], axis=0))


def once(*dims):
    return pl.BlockSpec(dims, lambda *_: (0,) * len(dims), pipeline_mode=pl.Buffered(1))


def window_pass(scalars, xs, us, ws):
    sizes = [16, 16, 32, 32, 32]
    dtypes = [jnp.bfloat16] * 5
    tile = pl.BlockSpec((4, 1, 2, WTOK, 128), lambda i, s: (0, i // 2, (i % 2) ^ s[0], 0, 0))
    part_specs = [
        pl.BlockSpec((2, 4, 1, 2, WTOK, 128), lambda i, s: (0, 0, i // 2, (i % 2) ^ s[0], 0, 0)), tile, tile,
    ]
    part_shapes = [
        shape((2, 4, 2, 4, WTOK, 128)), shape((4, 2, 4, WTOK, 128)), shape((4, 2, 4, WTOK, 128), jnp.float32),
    ]
    return pl.pallas_call(
        window_kernel,
        grid_spec=pltpu.PrefetchScalarGridSpec(
            num_scalar_prefetch=1,
            grid=(4,),
            in_specs=[
                pl.BlockSpec((4, 1, 2, HALF, 128), lambda i, s: (0, i // 2, (i % 2) ^ s[0], 0, 0))
            ] * 8 + [pl.BlockSpec((1, WTOK, D), lambda i, s: (i // 2, 0, 0))] * 4
            + [once(n, 128, 128) for n in (32, 32, 16, 32, 16)],
            out_specs=part_specs + [once(n, 128, 128) for n in sizes],
            scratch_shapes=[
                pltpu.VMEM((D, 768), jnp.bfloat16),
                pltpu.VMEM((256, D), jnp.bfloat16),
                pltpu.VMEM((4 * PAIR, D), jnp.bfloat16),
                pltpu.VMEM((256, D), jnp.float32),
                pltpu.VMEM((4 * PAIR, D), jnp.bfloat16),
                pltpu.VMEM((4 * PAIR, 768), jnp.bfloat16),
                pltpu.VMEM((1, 768), jnp.float32),
                pltpu.VMEM((4 * PAIR, 256), jnp.bfloat16),
            ],
        ),
        out_shape=part_shapes + [shape((n, 128, 128), t) for n, t in zip(sizes, dtypes)],
        compiler_params=pltpu.CompilerParams(vmem_limit_bytes=60 * MIB),
        cost_estimate=pl.CostEstimate(flops=32 * 10**9, bytes_accessed=30 * 10**6, transcendentals=10**6),
        name="window_pass",
    )(scalars, *xs, *us, *ws)


def after(values, *earlier):
    return lax.optimization_barrier(tuple(values) + earlier)[:len(values)]


def local(tokens, upstream, qkv_weight, out_weight):
    lon = lax.axis_index("lon")
    lat = lax.axis_index("lat")
    xh, y, c = lon // 8, (lon // 2) % 4, lon % 2
    last = (lat == lax.axis_size("lat") - 1).astype(jnp.int32)
    scalars = jnp.stack([jnp.int32(v) for v in (xh, c, y, last)])

    split, out_blocks = weight_split(scalars, qkv_weight, out_weight)
    token_low = hop_z(tokens[:6], -1)
    (upstream,) = after((upstream,), out_blocks)
    from_x = swap_x(jnp.stack([split[2], split[3]]))
    next_cols = next_lon(upstream[:, :3])

    cols = jnp.concatenate([upstream[:, 3:], next_cols], axis=1)
    cols = cols.reshape(2, 6, 2, WLON, LEVELS, D).transpose(0, 2, 1, 3, 4, 5)
    u_low, u_high = cols[0], cols[1]
    to_c, u_low, u_high, token_low = after(
        (jnp.stack([split[1], from_x[1]]), u_low, u_high, token_low), from_x, next_cols)
    from_c = swap_c(to_c)
    u_x = [swap_x(u_high)]
    u_low = hop_z(u_low, -1)
    pieces = token_split(scalars, tokens, token_low)
    pieces = [pieces[0]] + [shift_y(pieces[s], s) for s in (1, 2, 3)]
    x_high = jnp.stack([piece[0] for piece in pieces]).reshape(4, 2, 4, HALF, 128)
    x_low = jnp.stack([piece[1] for piece in pieces]).reshape(4, 2, 4, HALF, 128)

    shard = jnp.concatenate([split[0], from_x[0], from_c.reshape(12, 128, 128), out_blocks])
    shard, u_low, x_high, x_low = after((shard, u_low, x_high, x_low), from_c, u_low, u_x[0], *pieces[1:])
    w_up, w_down = shift_y(shard, 1), shift_y(shard, -1)
    u_x.append(across(u_low, True))
    u_own = [u_high, across(u_low, False)]
    highs = [x_high, swap_c(x_high), swap_x(x_high)]

    up_half, down_half, x_low = after(
        (w_up[:16], w_down[16:], x_low), w_up, w_down, u_x[1], u_own[1], highs[2])
    ws = [shard, w_up, shift_y(up_half, 1), w_down, shift_y(down_half, -1)]
    lows = [across(x_low, False), across(x_low, True)]
    u_own, u_x = (jnp.concatenate(u, axis=1).reshape(2, WTOK, D) for u in (u_own, u_x))
    us = [u_own, swap_c(u_own), u_x]

    lows[0], lows[1], to_c, u_x = after((*lows, highs[2], u_x), ws[2], ws[4], highs[1], us[1])
    us.append(swap_c(u_x))
    highs.append(swap_c(to_c))
    lows = [lows[0], swap_c(lows[0]), lows[1], swap_c(lows[1])]

    xs = highs + lows
    part_c, part_x, part_own, far_lo, far_hi, up, down, mine = window_pass(scalars, xs, us, ws)

    def plus(a, b):
        return (a.astype(jnp.float32) + b.astype(jnp.float32)).astype(jnp.bfloat16)

    got_c = swap_c(part_c)
    own = part_own + got_c[0].astype(jnp.float32)
    other = plus(part_x, got_c[1])

    far_lo, far_hi = shift_y(far_lo, -1), shift_y(far_hi, 1)
    low = [across(own[..., HALF:, :].astype(jnp.bfloat16), False), across(other[..., HALF:, :], True)]

    up = jnp.concatenate([plus(up[:16], far_lo), up[16:]])
    down = jnp.concatenate([down[:16], plus(down[16:], far_hi)])
    high, low, up, down = after(
        (other[..., :HALF, :], plus(*low), up, down), far_lo, far_hi, *low)
    high = (own[..., :HALF, :] + swap_x(high).astype(jnp.float32)).astype(jnp.bfloat16)
    low = hop_z(low, 1)
    up, down = shift_y(up, -1), shift_y(down, 1)

    total = mine.astype(jnp.float32) + up.astype(jnp.float32) + down.astype(jnp.float32)
    full, total = after((jnp.concatenate([high, low], axis=3), total), up, down)
    back = [full[0]] + [shift_y(full[s], -s) for s in (1, 2, 3)]
    blocks = total[:24].reshape(4, 6, 128, 128)
    sent = blocks.astype(jnp.bfloat16)
    by_x = swap_x(sent[2:])
    (near_x,) = after((by_x,), *back[1:])
    by_c = swap_c(jnp.stack([sent[1], near_x[1]]))
    grad_qkv_w = weight_join(scalars, total, by_c, by_x)
    grad_out_w = total[24:].reshape(8, 2, 64, 128).transpose(2, 0, 1, 3).reshape(64, D)

    result = token_join(scalars, [b.reshape(2, 4, WLAT, WLON, LEVELS, 128) for b in back])
    return (result, grad_qkv_w[None], grad_out_w[None])


def solution(mesh):
    return jax.shard_map(
        local,
        mesh=mesh,
        in_specs=(
            P("lat", None, None, "lon"),
            P("lat", "lon", None, None),
            P("lon", None),
            P("lon", None),
        ),
        out_specs=(P("lat", None, None, "lon"), P("lat", "lon", None), P("lat", "lon", None)),
        check_vma=False,
    )
```

```python
import functools

import jax
import jax.numpy as jnp
from jax import lax
from jax.experimental import pallas as pl
from jax.experimental.pallas import tpu as pltpu
from jax.sharding import PartitionSpec as P

HEAD_DIM = 64
WLAT = 12
WLON = 6
LEVELS = 2
WTOK = WLAT * WLON * LEVELS
PAIR = 2 * WTOK
HALF = WTOK // 2
D = 2048
NY = 4
MIB = 1024 * 1024

NEG_FILL = -1e30
EPSILON = 1e-05


def lon_of(xh, y, c):
    return (xh * NY + y) * 2 + c


COORDS = [(xh, y, c) for xh in range(2) for y in range(NY) for c in range(2)]


def swap_c(value):
    return lax.ppermute(value, "lon", [(lon_of(x, y, c), lon_of(x, y, 1 - c)) for x, y, c in COORDS])


def swap_x(value):
    return lax.ppermute(value, "lon", [(lon_of(x, y, c), lon_of(1 - x, y, c)) for x, y, c in COORDS])


def shift_y(value, by):
    return lax.ppermute(value, "lon", [(lon_of(x, y, c), lon_of(x, (y + by) % NY, c)) for x, y, c in COORDS])


def hop_z(value, by):
    rows, lons = lax.axis_size("lat"), lax.axis_size("lon")
    pairs = [
        (r * lons + i, (r + (2 * by if r % 2 == 0 else 0)) % rows * lons + i) for r in range(rows) for i in range(lons)
    ]
    return lax.ppermute(value, ("lat", "lon"), pairs)


def across(value, other):
    rows, lons = lax.axis_size("lat"), lax.axis_size("lon")
    pairs = [
        (r * lons + i, (r ^ 1) * lons + (lon_of(1 - i // 8, i // 2 % NY, i % 2) if other else i))
        for r in range(rows) for i in range(lons)
    ]
    return lax.ppermute(value, ("lat", "lon"), pairs)


def next_lon(value):
    return lax.ppermute(value, "lon", [(i, (i - 1) % 16) for i in range(16)])


def mm(a, b, dims):
    return lax.dot_general(a, b, (dims, ((), ())), preferred_element_type=jnp.float32)


def shape(dims, dtype=jnp.bfloat16):
    return jax.ShapeDtypeStruct(dims, dtype)


def whole(*dims):
    return pl.BlockSpec(dims, lambda *_: (0,) * len(dims))


def weight_split_kernel(s_ref, q_ref, o_ref, w_ref, out_ref):
    group = s_ref[0] * 2 + s_ref[1]
    for xh in range(2):
        for c in range(2):
            slot = group ^ (xh * 2 + c)
            for part in range(3):
                for pair in range(2):
                    lo = (part * 8 + xh * 4 + pair * 2) * 128 + c * 64
                    w_ref[slot, part * 2 + pair] = jnp.concatenate(
                        [q_ref[:, lo:lo + 64], q_ref[:, lo + 128:lo + 192]], axis=1)
    for i in range(8):
        out_ref[i] = jnp.concatenate(
            [o_ref[:, i * 256:i * 256 + 128], o_ref[:, i * 256 + 128:i * 256 + 256]], axis=0)


def weight_split(scalars, qkv_weight, out_weight):
    return pl.pallas_call(
        weight_split_kernel,
        grid_spec=pltpu.PrefetchScalarGridSpec(
            num_scalar_prefetch=1,
            grid=(1,),
            in_specs=[whole(128, 3072), whole(64, D)],
            out_specs=[whole(4, 6, 128, 128), whole(8, 128, 128)],
        ),
        out_shape=[shape((4, 6, 128, 128)), shape((8, 128, 128))],
        cost_estimate=pl.CostEstimate(flops=0, bytes_accessed=2 * 10**6, transcendentals=0),
        name="weight_split",
    )(scalars, qkv_weight, out_weight)


def weight_join_kernel(s_ref, a_ref, b_ref, c_ref, out_ref):
    group = s_ref[0] * 2 + s_ref[1]

    def block(slot, index):
        return jnp.where(slot == 0, a_ref[index], jnp.where(
            slot == 1, b_ref[0, index].astype(jnp.float32), jnp.where(
                slot == 3, b_ref[1, index], c_ref[0, index]).astype(jnp.float32)))

    for xh in range(2):
        slots = [group ^ (xh * 2), group ^ (xh * 2 + 1)]
        for part in range(3):
            for pair in range(2):
                left, right = (block(slot, part * 2 + pair) for slot in slots)
                lo = (part * 8 + xh * 4 + pair * 2) * 128
                out_ref[:, lo:lo + 128] = jnp.concatenate([left[:, :64], right[:, :64]], axis=1)
                out_ref[:, lo + 128:lo + 256] = jnp.concatenate([left[:, 64:], right[:, 64:]], axis=1)


def weight_join(scalars, own, by_c, by_x):
    return pl.pallas_call(
        weight_join_kernel,
        grid_spec=pltpu.PrefetchScalarGridSpec(
            num_scalar_prefetch=1,
            grid=(1,),
            in_specs=[whole(6, 128, 128), whole(2, 6, 128, 128), whole(2, 6, 128, 128)],
            out_specs=whole(128, 3072),
        ),
        out_shape=shape((128, 3072), jnp.float32),
        compiler_params=pltpu.CompilerParams(vmem_limit_bytes=60 * MIB),
        cost_estimate=pl.CostEstimate(flops=0, bytes_accessed=3 * 10**6, transcendentals=0),
        name="weight_join",
    )(scalars, own, by_c, by_x)


def spans(y):
    for s in range(4):
        for w in range(2):
            for t in range(4):
                xh, c = t // 2, t % 2
                start = 12 * lon_of(xh, lax.rem(y + s, 4), c) + 3 + 6 * w
                if xh == 1 and c == 1 and w == 1:
                    yield s, w, t, start, 0, 3
                    yield s, w, t, lax.rem(start + 3, 192), 3, 3
                else:
                    yield s, w, t, start, 0, 6


def token_split_kernel(s_ref, high_ref, low_ref, *outs):
    for s, w, t, start, offset, columns in spans(s_ref[2]):
        for half, ref in enumerate((high_ref, low_ref)):
            outs[s][half, w, t, :, offset:offset + columns] = ref[:, pl.ds(start, columns)]


def token_split(scalars, tokens, low):
    dims = (2, 2, 4, 6, WLON, LEVELS, 128)
    return pl.pallas_call(
        token_split_kernel,
        grid_spec=pltpu.PrefetchScalarGridSpec(
            num_scalar_prefetch=1,
            grid=(1,),
            in_specs=[
                pl.BlockSpec((6, 192, LEVELS, 128), lambda i, r: (1, 0, 0, 0)), whole(6, 192, LEVELS, 128),
            ],
            out_specs=[whole(*dims)] * 4,
        ),
        out_shape=[shape(dims)] * 4,
        compiler_params=pltpu.CompilerParams(vmem_limit_bytes=40 * MIB),
        cost_estimate=pl.CostEstimate(flops=0, bytes_accessed=3 * 10**6, transcendentals=0),
        name="token_split",
    )(scalars, tokens, low)


def token_join_kernel(s_ref, *refs):
    parts, out_ref = refs[:4], refs[4]
    for s, w, t, start, offset, columns in spans(s_ref[2]):
        out_ref[6:12, pl.ds(start, columns)] = parts[s][w, t, 0:6, offset:offset + columns]
        out_ref[0:6, pl.ds(start, columns)] = parts[s][w, t, 6:12, offset:offset + columns]


def token_join(scalars, parts):
    return pl.pallas_call(
        token_join_kernel,
        grid_spec=pltpu.PrefetchScalarGridSpec(
            num_scalar_prefetch=1,
            grid=(1,),
            in_specs=[whole(2, 4, WLAT, WLON, LEVELS, 128)] * 4,
            out_specs=whole(WLAT, 192, LEVELS, 128),
        ),
        out_shape=shape((WLAT, 192, LEVELS, 128)),
        compiler_params=pltpu.CompilerParams(vmem_limit_bytes=40 * MIB),
        cost_estimate=pl.CostEstimate(flops=0, bytes_accessed=3 * 10**6, transcendentals=0),
        name="token_join",
    )(scalars, *parts)


def attend(qkv, grad_att, split):
    scale = HEAD_DIM ** -0.5
    lane = lax.broadcasted_iota(jnp.int32, (1, 128), 1)
    row_group = lax.broadcasted_iota(jnp.int32, (WTOK, WTOK), 0) >= HALF
    col_group = lax.broadcasted_iota(jnp.int32, (WTOK, WTOK), 1) >= HALF
    keep = (row_group == col_group) | (split == 0)
    units = []
    for w in range(2):
        rows = slice(w * WTOK, (w + 1) * WTOK)
        for pair in range(2):
            cols = slice(pair * 128, (pair + 1) * 128)
            q = qkv[rows, 0:256][:, cols] * scale
            k = qkv[rows, 256:512][:, cols]
            v = qkv[rows, 512:768][:, cols]
            g = grad_att[rows, cols]
            heads = []
            for h in range(2):
                mine = (lane < 64) == (h == 0)
                heads.append((
                    jnp.where(mine, q, 0.0).astype(jnp.bfloat16),
                    jnp.where(mine, g, 0.0).astype(jnp.bfloat16),
                ))
            kb, vb = k.astype(jnp.bfloat16), v.astype(jnp.bfloat16)
            units.append((heads, kb, vb, k.T.astype(jnp.bfloat16), v.T.astype(jnp.bfloat16)))
    work = [(u, h) for u in range(4) for h in range(2)]
    scores = {
        (u, h): mm(units[u][1], units[u][0][h][0], ((1,), (1,))) for u, h in work
    }
    probs, probs_b = {}, {}
    for key in work:
        kept = jnp.where(keep, scores[key], NEG_FILL)
        expons = jnp.exp(kept - jnp.max(kept, axis=0, keepdims=True))
        probs[key] = expons * (1.0 / jnp.sum(expons, axis=0, keepdims=True))
        probs_b[key] = probs[key].astype(jnp.bfloat16)
    grads = {}
    for u, h in work:
        weighted = probs[u, h] * mm(units[u][2], units[u][0][h][1], ((1,), (1,)))
        inner = jnp.sum(weighted, axis=0, keepdims=True)
        grads[u, h] = (weighted - probs[u, h] * inner).astype(jnp.bfloat16)
    att, dq, dk, dv = [], [], [], []
    for u in range(4):
        heads, _, _, kt, vt = units[u]
        att.append(jnp.concatenate(
            [mm(vt[h * 64:(h + 1) * 64], probs_b[u, h], ((1,), (0,))) for h in range(2)], axis=0).T)
        dq.append(jnp.concatenate(
            [mm(kt[h * 64:(h + 1) * 64], grads[u, h], ((1,), (0,))) for h in range(2)], axis=0).T * scale)
        dk.append(sum(mm(grads[u, h], heads[h][0], ((1,), (0,))) for h in range(2)))
        dv.append(sum(mm(probs_b[u, h], heads[h][1], ((1,), (0,))) for h in range(2)))
    attended = jnp.concatenate([jnp.concatenate(att[2 * w:2 * w + 2], axis=1) for w in range(2)], axis=0)
    dqkv = jnp.concatenate([
        jnp.concatenate(dq[2 * w:2 * w + 2] + dk[2 * w:2 * w + 2] + dv[2 * w:2 * w + 2], axis=1)
        for w in range(2)], axis=0)
    return attended.astype(jnp.bfloat16), dqkv.astype(jnp.bfloat16)


ORDER = (2, 1, 3, 0)


def window_kernel(s_ref, *refs):
    highs, lows, us, ws = refs[:4], refs[4:8], refs[8:12], refs[12:17]
    pc_ref, px_ref, po_ref = refs[17:20]
    terms = refs[20:25]
    wfull, wout, ub, gacc, nb_all, dq_all, wsum, att_all = refs[25:]
    i = pl.program_id(0)
    c, y = s_ref[1], s_ref[2]

    @pl.when(i == 0)
    def _():
        for s in range(4):
            def block(index):
                if s == 2:
                    return ws[2][index] if index < 16 else ws[4][index - 16]
                return ws[s][index]
            for k in range(4):
                row = (s * 4 + k) * 128
                for part in range(6):
                    wfull[row:row + 128, part * 128:(part + 1) * 128] = block((0, 2, 1, 3)[k] * 6 + part)
            head = lax.rem(y + 4 - s, 4)
            rows = pl.ds(pl.multiple_of(head * 64, 64), 64)
            for j in range(8):
                wout[rows, j * 256:j * 256 + 128] = block(24 + j)[0:64]
                wout[rows, j * 256 + 128:j * 256 + 256] = block(24 + j)[64:128]
        wsum[...] = jnp.sum(wfull[...].astype(jnp.float32), axis=0, keepdims=True)

    rows = pl.ds(pl.multiple_of(i * PAIR, PAIR), PAIR)
    for step in range(4):
        @pl.when(i == step)
        def _():
            for dc in range(2):
                ub[pl.ds(pl.multiple_of(step * PAIR + (dc ^ c) * WTOK, WTOK), WTOK), :] = us[2 * (step % 2) + dc][0]

    x = jnp.concatenate([
        jnp.concatenate(
            [half[k][s, 0].astype(jnp.float32) for half in (highs, lows)], axis=1).reshape(PAIR, 128)
        for s in range(4) for k in range(4)
    ], axis=1)
    centred = x - jnp.mean(x, axis=-1, keepdims=True)
    inverse = lax.rsqrt(jnp.mean(centred * centred, axis=-1, keepdims=True) + EPSILON)
    nb = (centred * inverse).astype(jnp.bfloat16)
    nb_all[rows, :] = nb
    qkv = mm(nb, wfull[...], ((1,), (0,)))
    grad_att = mm(ub[rows, :], wout[...], ((1,), (1,)))
    attended, dqkv = attend(qkv, grad_att, s_ref[3])
    att_all[rows, :] = attended
    dq_all[rows, :] = dqkv
    dqkv_f = dqkv.astype(jnp.float32)
    mean_one = jnp.sum(dqkv_f * wsum[...], axis=-1, keepdims=True) * (inverse / D)
    mean_two = jnp.sum(dqkv_f * qkv, axis=-1, keepdims=True) * (inverse / D)
    grad_normal = mm(dqkv, wfull[...], ((1,), (1,)))
    normal = nb_all[rows, :].astype(jnp.float32)
    grad_rolled = inverse * grad_normal - mean_one - normal * mean_two

    for s in range(4):
        part = [grad_rolled[:, (s * 4 + k) * 128:(s * 4 + k + 1) * 128].reshape(2, WTOK, 128) for k in range(4)]
        pc_ref[0, s, 0] = part[1].astype(jnp.bfloat16)
        pc_ref[1, s, 0] = part[3].astype(jnp.bfloat16)
        px_ref[s, 0] = part[2].astype(jnp.bfloat16)
        block = lon_of(s_ref[0], lax.rem(y + 4 - s, 4), c)
        own = ub[rows, pl.ds(pl.multiple_of(block * 128, 128), 128)].astype(jnp.float32)
        po_ref[s, 0] = (part[0] + own.reshape(2, WTOK, 128)).astype(jnp.bfloat16)

    @pl.when(i == 3)
    def _():
        gacc[...] = mm(att_all[...], ub[...], ((0,), (0,)))
        for step, s in enumerate(ORDER):
            places = {2: ((0, 0), (1, 16)), 1: ((2, 0), (0, 16)), 3: ((1, 0), (3, 0)), 0: ((4, 0), (4, 16))}[s]

            def put(index, value):
                at, offset = places[index // 16]
                terms[at][offset + index % 16] = value.astype(jnp.bfloat16)

            term = mm(nb_all[:, s * 512:(s + 1) * 512], dq_all[...], ((0,), (0,)))
            for k in range(4):
                for part in range(6):
                    put(k * 6 + part, term[k * 128:(k + 1) * 128, part * 128:(part + 1) * 128])
            head = lax.rem(y + 4 - s, 4)
            gw = gacc[pl.ds(pl.multiple_of(head * 64, 64), 64), :]
            for j in range(8):
                put(24 + j, jnp.concatenate(
                    [gw[:, j * 256:j * 256 + 128], gw[:, j * 256 + 128:j * 256 + 256]], axis=0))


def once(*dims):
    return pl.BlockSpec(dims, lambda *_: (0,) * len(dims), pipeline_mode=pl.Buffered(1))


def window_pass(scalars, xs, us, ws):
    sizes = [32, 32, 16, 16, 32]
    dtypes = [jnp.bfloat16] * 5
    tile = pl.BlockSpec((4, 1, 2, WTOK, 128), lambda i, s: (0, i // 2, (i % 2) ^ s[0], 0, 0))
    part_specs = [
        pl.BlockSpec((2, 4, 1, 2, WTOK, 128), lambda i, s: (0, 0, i // 2, (i % 2) ^ s[0], 0, 0)), tile, tile,
    ]
    part_shapes = [
        shape((2, 4, 2, 4, WTOK, 128)), shape((4, 2, 4, WTOK, 128)), shape((4, 2, 4, WTOK, 128)),
    ]
    return pl.pallas_call(
        window_kernel,
        grid_spec=pltpu.PrefetchScalarGridSpec(
            num_scalar_prefetch=1,
            grid=(4,),
            in_specs=[
                pl.BlockSpec((4, 1, 2, HALF, 128), lambda i, s: (0, i // 2, (i % 2) ^ s[0], 0, 0))
            ] * 8 + [pl.BlockSpec((1, WTOK, D), lambda i, s: (i // 2, 0, 0))] * 4
            + [once(n, 128, 128) for n in (32, 32, 16, 32, 16)],
            out_specs=part_specs + [once(n, 128, 128) for n in sizes],
            scratch_shapes=[
                pltpu.VMEM((D, 768), jnp.bfloat16),
                pltpu.VMEM((256, D), jnp.bfloat16),
                pltpu.VMEM((4 * PAIR, D), jnp.bfloat16),
                pltpu.VMEM((256, D), jnp.float32),
                pltpu.VMEM((4 * PAIR, D), jnp.bfloat16),
                pltpu.VMEM((4 * PAIR, 768), jnp.bfloat16),
                pltpu.VMEM((1, 768), jnp.float32),
                pltpu.VMEM((4 * PAIR, 256), jnp.bfloat16),
            ],
        ),
        out_shape=part_shapes + [shape((n, 128, 128), t) for n, t in zip(sizes, dtypes)],
        compiler_params=pltpu.CompilerParams(vmem_limit_bytes=40 * MIB),
        cost_estimate=pl.CostEstimate(flops=32 * 10**9, bytes_accessed=30 * 10**6, transcendentals=10**6),
        name="window_pass",
    )(scalars, *xs, *us, *ws)


def after(values, *earlier):
    return lax.optimization_barrier(tuple(values) + earlier)[:len(values)]


def local(tokens, upstream, qkv_weight, out_weight):
    lon = lax.axis_index("lon")
    lat = lax.axis_index("lat")
    xh, y, c = lon // 8, (lon // 2) % 4, lon % 2
    last = (lat == lax.axis_size("lat") - 1).astype(jnp.int32)
    scalars = jnp.stack([jnp.int32(v) for v in (xh, c, y, last)])

    split, out_blocks = weight_split(scalars, qkv_weight, out_weight)
    token_low = hop_z(tokens[:6], -1)
    (upstream,) = after((upstream,), out_blocks)
    from_x = swap_x(jnp.stack([split[2], split[3]]))
    next_cols = next_lon(upstream[:, :3])

    cols = jnp.concatenate([upstream[:, 3:], next_cols], axis=1)
    cols = cols.reshape(2, 6, 2, WLON, LEVELS, D).transpose(0, 2, 1, 3, 4, 5).reshape(2, 2, HALF, D)
    pieces = token_split(scalars, tokens, token_low)
    u_low, u_high, *pieces = after((cols[0], cols[1], *pieces))
    from_c = swap_c(jnp.stack([split[1], from_x[1]]))
    u_x = [swap_x(u_high)]
    u_low = hop_z(u_low, -1)
    pieces = [pieces[0]] + [shift_y(pieces[s], s) for s in (1, 2, 3)]
    x_high = jnp.stack([piece[0] for piece in pieces]).reshape(4, 2, 4, HALF, 128)
    x_low = jnp.stack([piece[1] for piece in pieces]).reshape(4, 2, 4, HALF, 128)

    shard = jnp.concatenate([split[0], from_x[0], from_c.reshape(12, 128, 128), out_blocks])
    shard, u_low, x_high, x_low = after((shard, u_low, x_high, x_low), from_c, u_low, u_x[0], *pieces[1:])
    w_up, w_down = shift_y(shard, 1), shift_y(shard, -1)
    u_x.append(across(u_low, True))
    u_own = [u_high, across(u_low, False)]
    highs = [x_high, swap_c(x_high), swap_x(x_high)]

    up_half, down_half, x_low = after(
        (w_up[:16], w_down[16:], x_low), w_up, w_down, u_x[1], u_own[1], highs[2])
    ws = [shard, w_up, shift_y(up_half, 1), w_down, shift_y(down_half, -1)]
    lows = [across(x_low, False), across(x_low, True)]
    u_own, u_x = (jnp.concatenate(u, axis=1) for u in (u_own, u_x))
    us = [u_own, swap_c(u_own), u_x]

    lows[0], lows[1], to_c, u_x = after((*lows, highs[2], u_x), ws[2], ws[4], highs[1], us[1])
    us.append(swap_c(u_x))
    highs.append(swap_c(to_c))
    lows = [lows[0], swap_c(lows[0]), lows[1], swap_c(lows[1])]

    xs = highs + lows
    part_c, part_x, part_own, lower, upper, up, down, mine = window_pass(scalars, xs, us, ws)

    def plus(a, b):
        return (a.astype(jnp.float32) + b.astype(jnp.float32)).astype(jnp.bfloat16)

    got_c = swap_c(part_c)
    own = part_own.astype(jnp.float32) + got_c[0].astype(jnp.float32)
    other = plus(part_x, got_c[1])

    lower, upper = shift_y(lower, -1), shift_y(upper, 1)
    low = [across(own[..., HALF:, :].astype(jnp.bfloat16), False), across(other[..., HALF:, :], True)]

    high, low = after((other[..., :HALF, :], plus(*low)), *low)
    up, down = after((plus(up, lower[:16]), plus(down, upper[16:])), lower, upper, high, low)
    high = (own[..., :HALF, :] + swap_x(high).astype(jnp.float32)).astype(jnp.bfloat16)
    low = hop_z(low, 1)
    up, down = shift_y(up, -1), shift_y(down, 1)

    total = mine.astype(jnp.float32) + jnp.concatenate([up, lower[16:]]).astype(jnp.float32) + jnp.concatenate(
        [upper[:16], down]).astype(jnp.float32)
    full = jnp.concatenate([high, low], axis=3)
    (total,) = after((total,), full)
    back = [full[0]] + [shift_y(full[s], -s) for s in (1, 2, 3)]
    blocks = total[:24].reshape(4, 6, 128, 128)
    sent = blocks.astype(jnp.bfloat16)
    by_x = swap_x(sent[2:])
    (near_x,) = after((by_x,), *back[1:])
    by_c = swap_c(jnp.stack([sent[1], near_x[1]]))
    grad_qkv_w = weight_join(scalars, total, by_c, by_x)
    grad_out_w = total[24:].reshape(8, 2, 64, 128).transpose(2, 0, 1, 3).reshape(64, D)

    result = token_join(scalars, [b.reshape(2, 4, WLAT, WLON, LEVELS, 128) for b in back])
    return (result, grad_qkv_w[None], grad_out_w[None])


def solution(mesh):
    return jax.shard_map(
        local,
        mesh=mesh,
        in_specs=(
            P("lat", None, None, "lon"),
            P("lat", "lon", None, None),
            P("lon", None),
            P("lon", None),
        ),
        out_specs=(P("lat", None, None, "lon"), P("lat", "lon", None), P("lat", "lon", None)),
        check_vma=False,
    )
```

```python
import functools

import jax
import jax.numpy as jnp
from jax import lax
from jax.experimental import pallas as pl
from jax.experimental.pallas import tpu as pltpu
from jax.sharding import PartitionSpec as P

HEAD_DIM = 64
WLAT = 12
WLON = 6
LEVELS = 2
WTOK = WLAT * WLON * LEVELS
PAIR = 2 * WTOK
HALF = WTOK // 2
D = 2048
NY = 4
MIB = 1024 * 1024

NEG_FILL = -1e30
EPSILON = 1e-05


def lon_of(xh, y, c):
    return (xh * NY + y) * 2 + c


COORDS = [(xh, y, c) for xh in range(2) for y in range(NY) for c in range(2)]


def swap_c(value):
    return lax.ppermute(value, "lon", [(lon_of(x, y, c), lon_of(x, y, 1 - c)) for x, y, c in COORDS])


def swap_x(value):
    return lax.ppermute(value, "lon", [(lon_of(x, y, c), lon_of(1 - x, y, c)) for x, y, c in COORDS])


def shift_y(value, by):
    return lax.ppermute(value, "lon", [(lon_of(x, y, c), lon_of(x, (y + by) % NY, c)) for x, y, c in COORDS])


def hop_z(value, by):
    rows, lons = lax.axis_size("lat"), lax.axis_size("lon")
    pairs = [
        (r * lons + i, (r + (2 * by if r % 2 == 0 else 0)) % rows * lons + i) for r in range(rows) for i in range(lons)
    ]
    return lax.ppermute(value, ("lat", "lon"), pairs)


def across(value, other):
    rows, lons = lax.axis_size("lat"), lax.axis_size("lon")
    pairs = [
        (r * lons + i, (r ^ 1) * lons + (lon_of(1 - i // 8, i // 2 % NY, i % 2) if other else i))
        for r in range(rows) for i in range(lons)
    ]
    return lax.ppermute(value, ("lat", "lon"), pairs)


def next_lon(value):
    return lax.ppermute(value, "lon", [(i, (i - 1) % 16) for i in range(16)])


def mm(a, b, dims):
    return lax.dot_general(a, b, (dims, ((), ())), preferred_element_type=jnp.float32)


def shape(dims, dtype=jnp.bfloat16):
    return jax.ShapeDtypeStruct(dims, dtype)


def whole(*dims):
    return pl.BlockSpec(dims, lambda *_: (0,) * len(dims))


def weight_split_kernel(s_ref, q_ref, o_ref, w_ref, out_ref):
    group = s_ref[0] * 2 + s_ref[1]
    for xh in range(2):
        for c in range(2):
            slot = group ^ (xh * 2 + c)
            for part in range(3):
                for pair in range(2):
                    lo = (part * 8 + xh * 4 + pair * 2) * 128 + c * 64
                    w_ref[slot, part * 2 + pair] = jnp.concatenate(
                        [q_ref[:, lo:lo + 64], q_ref[:, lo + 128:lo + 192]], axis=1)
    for i in range(8):
        out_ref[i] = jnp.concatenate(
            [o_ref[:, i * 256:i * 256 + 128], o_ref[:, i * 256 + 128:i * 256 + 256]], axis=0)


def weight_split(scalars, qkv_weight, out_weight):
    return pl.pallas_call(
        weight_split_kernel,
        grid_spec=pltpu.PrefetchScalarGridSpec(
            num_scalar_prefetch=1,
            grid=(1,),
            in_specs=[whole(128, 3072), whole(64, D)],
            out_specs=[whole(4, 6, 128, 128), whole(8, 128, 128)],
        ),
        out_shape=[shape((4, 6, 128, 128)), shape((8, 128, 128))],
        cost_estimate=pl.CostEstimate(flops=0, bytes_accessed=2 * 10**6, transcendentals=0),
        name="weight_split",
    )(scalars, qkv_weight, out_weight)


def weight_join_kernel(s_ref, a_ref, b_ref, c_ref, out_ref):
    group = s_ref[0] * 2 + s_ref[1]

    def block(slot, index):
        return jnp.where(slot == 0, a_ref[index], jnp.where(
            slot == 1, b_ref[0, index].astype(jnp.float32), jnp.where(
                slot == 3, b_ref[1, index], c_ref[0, index]).astype(jnp.float32)))

    for xh in range(2):
        slots = [group ^ (xh * 2), group ^ (xh * 2 + 1)]
        for part in range(3):
            for pair in range(2):
                left, right = (block(slot, part * 2 + pair) for slot in slots)
                lo = (part * 8 + xh * 4 + pair * 2) * 128
                out_ref[:, lo:lo + 128] = jnp.concatenate([left[:, :64], right[:, :64]], axis=1)
                out_ref[:, lo + 128:lo + 256] = jnp.concatenate([left[:, 64:], right[:, 64:]], axis=1)


def weight_join(scalars, own, by_c, by_x):
    return pl.pallas_call(
        weight_join_kernel,
        grid_spec=pltpu.PrefetchScalarGridSpec(
            num_scalar_prefetch=1,
            grid=(1,),
            in_specs=[whole(6, 128, 128), whole(2, 6, 128, 128), whole(2, 6, 128, 128)],
            out_specs=whole(128, 3072),
        ),
        out_shape=shape((128, 3072), jnp.float32),
        compiler_params=pltpu.CompilerParams(vmem_limit_bytes=60 * MIB),
        cost_estimate=pl.CostEstimate(flops=0, bytes_accessed=3 * 10**6, transcendentals=0),
        name="weight_join",
    )(scalars, own, by_c, by_x)


def spans(y):
    for s in range(4):
        for w in range(2):
            for t in range(4):
                xh, c = t // 2, t % 2
                start = 12 * lon_of(xh, lax.rem(y + s, 4), c) + 3 + 6 * w
                if xh == 1 and c == 1 and w == 1:
                    yield s, w, t, start, 0, 3
                    yield s, w, t, lax.rem(start + 3, 192), 3, 3
                else:
                    yield s, w, t, start, 0, 6


def token_split_kernel(s_ref, high_ref, low_ref, *outs):
    for s, w, t, start, offset, columns in spans(s_ref[2]):
        for half, ref in enumerate((high_ref, low_ref)):
            outs[s][half, w, t, :, offset:offset + columns] = ref[:, pl.ds(start, columns)]


def token_split(scalars, tokens, low):
    dims = (2, 2, 4, 6, WLON, LEVELS, 128)
    return pl.pallas_call(
        token_split_kernel,
        grid_spec=pltpu.PrefetchScalarGridSpec(
            num_scalar_prefetch=1,
            grid=(1,),
            in_specs=[
                pl.BlockSpec((6, 192, LEVELS, 128), lambda i, r: (1, 0, 0, 0)), whole(6, 192, LEVELS, 128),
            ],
            out_specs=[whole(*dims)] * 4,
        ),
        out_shape=[shape(dims)] * 4,
        compiler_params=pltpu.CompilerParams(vmem_limit_bytes=40 * MIB),
        cost_estimate=pl.CostEstimate(flops=0, bytes_accessed=3 * 10**6, transcendentals=0),
        name="token_split",
    )(scalars, tokens, low)


def token_join_kernel(s_ref, *refs):
    parts, out_ref = refs[:4], refs[4]
    for s, w, t, start, offset, columns in spans(s_ref[2]):
        out_ref[6:12, pl.ds(start, columns)] = parts[s][w, t, 0:6, offset:offset + columns]
        out_ref[0:6, pl.ds(start, columns)] = parts[s][w, t, 6:12, offset:offset + columns]


def token_join(scalars, parts):
    return pl.pallas_call(
        token_join_kernel,
        grid_spec=pltpu.PrefetchScalarGridSpec(
            num_scalar_prefetch=1,
            grid=(1,),
            in_specs=[whole(2, 4, WLAT, WLON, LEVELS, 128)] * 4,
            out_specs=whole(WLAT, 192, LEVELS, 128),
        ),
        out_shape=shape((WLAT, 192, LEVELS, 128)),
        compiler_params=pltpu.CompilerParams(vmem_limit_bytes=40 * MIB),
        cost_estimate=pl.CostEstimate(flops=0, bytes_accessed=3 * 10**6, transcendentals=0),
        name="token_join",
    )(scalars, *parts)


def attend(qkv, grad_att, split):
    scale = HEAD_DIM ** -0.5
    lane = lax.broadcasted_iota(jnp.int32, (1, 128), 1)
    row_group = lax.broadcasted_iota(jnp.int32, (WTOK, WTOK), 0) >= HALF
    col_group = lax.broadcasted_iota(jnp.int32, (WTOK, WTOK), 1) >= HALF
    keep = (row_group == col_group) | (split == 0)
    units = []
    for w in range(2):
        rows = slice(w * WTOK, (w + 1) * WTOK)
        for pair in range(2):
            cols = slice(pair * 128, (pair + 1) * 128)
            q = qkv[rows, 0:256][:, cols] * scale
            k = qkv[rows, 256:512][:, cols]
            v = qkv[rows, 512:768][:, cols]
            g = grad_att[rows, cols]
            heads = []
            for h in range(2):
                mine = (lane < 64) == (h == 0)
                heads.append((
                    jnp.where(mine, q, 0.0).astype(jnp.bfloat16),
                    jnp.where(mine, g, 0.0).astype(jnp.bfloat16),
                ))
            kb, vb = k.astype(jnp.bfloat16), v.astype(jnp.bfloat16)
            units.append((heads, kb, vb, k.T.astype(jnp.bfloat16), v.T.astype(jnp.bfloat16)))
    work = [(u, h) for u in range(4) for h in range(2)]
    scores = {
        (u, h): mm(units[u][1], units[u][0][h][0], ((1,), (1,))) for u, h in work
    }
    probs, probs_b = {}, {}
    for key in work:
        kept = jnp.where(keep, scores[key], NEG_FILL)
        expons = jnp.exp(kept - jnp.max(kept, axis=0, keepdims=True))
        probs[key] = expons * (1.0 / jnp.sum(expons, axis=0, keepdims=True))
        probs_b[key] = probs[key].astype(jnp.bfloat16)
    grads = {}
    for u, h in work:
        weighted = probs[u, h] * mm(units[u][2], units[u][0][h][1], ((1,), (1,)))
        inner = jnp.sum(weighted, axis=0, keepdims=True)
        grads[u, h] = (weighted - probs[u, h] * inner).astype(jnp.bfloat16)
    att, dq, dk, dv = [], [], [], []
    for u in range(4):
        heads, _, _, kt, vt = units[u]
        att.append(jnp.concatenate(
            [mm(vt[h * 64:(h + 1) * 64], probs_b[u, h], ((1,), (0,))) for h in range(2)], axis=0).T)
        dq.append(jnp.concatenate(
            [mm(kt[h * 64:(h + 1) * 64], grads[u, h], ((1,), (0,))) for h in range(2)], axis=0).T * scale)
        dk.append(sum(mm(grads[u, h], heads[h][0], ((1,), (0,))) for h in range(2)))
        dv.append(sum(mm(probs_b[u, h], heads[h][1], ((1,), (0,))) for h in range(2)))
    attended = jnp.concatenate([jnp.concatenate(att[2 * w:2 * w + 2], axis=1) for w in range(2)], axis=0)
    dqkv = jnp.concatenate([
        jnp.concatenate(dq[2 * w:2 * w + 2] + dk[2 * w:2 * w + 2] + dv[2 * w:2 * w + 2], axis=1)
        for w in range(2)], axis=0)
    return attended.astype(jnp.bfloat16), dqkv.astype(jnp.bfloat16)


ORDER = (2, 1, 3, 0)


def window_kernel(s_ref, *refs):
    highs, lows, us, ws = refs[:4], refs[4:8], refs[8:12], refs[12:17]
    pc_ref, px_ref, po_ref = refs[17:20]
    terms = refs[20:25]
    wfull, wout, ub, gacc, nb_all, dq_all, wsum, att_all = refs[25:]
    i = pl.program_id(0)
    c, y = s_ref[1], s_ref[2]

    @pl.when(i == 0)
    def _():
        for s in range(4):
            def block(index):
                if s == 2:
                    return ws[2][index] if index < 16 else ws[4][index - 16]
                return ws[s][index]
            for k in range(4):
                row = (s * 4 + k) * 128
                for part in range(6):
                    wfull[row:row + 128, part * 128:(part + 1) * 128] = block((0, 2, 1, 3)[k] * 6 + part)
            head = lax.rem(y + 4 - s, 4)
            rows = pl.ds(pl.multiple_of(head * 64, 64), 64)
            for j in range(8):
                wout[rows, j * 256:j * 256 + 128] = block(24 + j)[0:64]
                wout[rows, j * 256 + 128:j * 256 + 256] = block(24 + j)[64:128]
        wsum[...] = jnp.sum(wfull[...].astype(jnp.float32), axis=0, keepdims=True)

    rows = pl.ds(pl.multiple_of(i * PAIR, PAIR), PAIR)
    for step in range(4):
        @pl.when(i == step)
        def _():
            for dc in range(2):
                ub[pl.ds(pl.multiple_of(step * PAIR + (dc ^ c) * WTOK, WTOK), WTOK), :] = us[2 * (step % 2) + dc][0]

    x = jnp.concatenate([
        jnp.concatenate(
            [half[k][s, 0].astype(jnp.float32) for half in (highs, lows)], axis=1).reshape(PAIR, 128)
        for s in range(4) for k in range(4)
    ], axis=1)
    centred = x - jnp.mean(x, axis=-1, keepdims=True)
    inverse = lax.rsqrt(jnp.mean(centred * centred, axis=-1, keepdims=True) + EPSILON)
    nb = (centred * inverse).astype(jnp.bfloat16)
    nb_all[rows, :] = nb
    qkv = mm(nb, wfull[...], ((1,), (0,)))
    grad_att = mm(ub[rows, :], wout[...], ((1,), (1,)))
    attended, dqkv = attend(qkv, grad_att, s_ref[3])
    att_all[rows, :] = attended
    dq_all[rows, :] = dqkv
    dqkv_f = dqkv.astype(jnp.float32)
    mean_one = jnp.sum(dqkv_f * wsum[...], axis=-1, keepdims=True) * (inverse / D)
    mean_two = jnp.sum(dqkv_f * qkv, axis=-1, keepdims=True) * (inverse / D)
    grad_normal = mm(dqkv, wfull[...], ((1,), (1,)))
    normal = nb_all[rows, :].astype(jnp.float32)
    grad_rolled = inverse * grad_normal - mean_one - normal * mean_two

    for s in range(4):
        part = [grad_rolled[:, (s * 4 + k) * 128:(s * 4 + k + 1) * 128].reshape(2, WTOK, 128) for k in range(4)]
        pc_ref[0, s, 0] = part[1].astype(jnp.bfloat16)
        pc_ref[1, s, 0] = part[3].astype(jnp.bfloat16)
        px_ref[s, 0] = part[2].astype(jnp.bfloat16)
        block = lon_of(s_ref[0], lax.rem(y + 4 - s, 4), c)
        own = ub[rows, pl.ds(pl.multiple_of(block * 128, 128), 128)].astype(jnp.float32)
        po_ref[s, 0] = (part[0] + own.reshape(2, WTOK, 128)).astype(jnp.bfloat16)

    @pl.when(i == 3)
    def _():
        gacc[...] = mm(att_all[...], ub[...], ((0,), (0,)))
        for step, s in enumerate(ORDER):
            places = {2: ((0, 0), (1, 16)), 1: ((2, 0), (0, 16)), 3: ((1, 0), (3, 0)), 0: ((4, 0), (4, 16))}[s]

            def put(index, value):
                at, offset = places[index // 16]
                terms[at][offset + index % 16] = value.astype(jnp.bfloat16)

            term = mm(nb_all[:, s * 512:(s + 1) * 512], dq_all[...], ((0,), (0,)))
            for k in range(4):
                for part in range(6):
                    put(k * 6 + part, term[k * 128:(k + 1) * 128, part * 128:(part + 1) * 128])
            head = lax.rem(y + 4 - s, 4)
            gw = gacc[pl.ds(pl.multiple_of(head * 64, 64), 64), :]
            for j in range(8):
                put(24 + j, jnp.concatenate(
                    [gw[:, j * 256:j * 256 + 128], gw[:, j * 256 + 128:j * 256 + 256]], axis=0))


def once(*dims):
    return pl.BlockSpec(dims, lambda *_: (0,) * len(dims), pipeline_mode=pl.Buffered(1))


def window_pass(scalars, xs, us, ws):
    sizes = [32, 32, 16, 16, 32]
    dtypes = [jnp.bfloat16] * 5
    tile = pl.BlockSpec((4, 1, 2, WTOK, 128), lambda i, s: (0, i // 2, (i % 2) ^ s[0], 0, 0))
    part_specs = [
        pl.BlockSpec((2, 4, 1, 2, WTOK, 128), lambda i, s: (0, 0, i // 2, (i % 2) ^ s[0], 0, 0)), tile, tile,
    ]
    part_shapes = [
        shape((2, 4, 2, 4, WTOK, 128)), shape((4, 2, 4, WTOK, 128)), shape((4, 2, 4, WTOK, 128)),
    ]
    return pl.pallas_call(
        window_kernel,
        grid_spec=pltpu.PrefetchScalarGridSpec(
            num_scalar_prefetch=1,
            grid=(4,),
            in_specs=[
                pl.BlockSpec((4, 1, 2, HALF, 128), lambda i, s: (0, i // 2, (i % 2) ^ s[0], 0, 0))
            ] * 8 + [pl.BlockSpec((1, WTOK, D), lambda i, s: (i // 2, 0, 0))] * 4
            + [once(n, 128, 128) for n in (32, 32, 16, 32, 16)],
            out_specs=part_specs + [once(n, 128, 128) for n in sizes],
            scratch_shapes=[
                pltpu.VMEM((D, 768), jnp.bfloat16),
                pltpu.VMEM((256, D), jnp.bfloat16),
                pltpu.VMEM((4 * PAIR, D), jnp.bfloat16),
                pltpu.VMEM((256, D), jnp.float32),
                pltpu.VMEM((4 * PAIR, D), jnp.bfloat16),
                pltpu.VMEM((4 * PAIR, 768), jnp.bfloat16),
                pltpu.VMEM((1, 768), jnp.float32),
                pltpu.VMEM((4 * PAIR, 256), jnp.bfloat16),
            ],
        ),
        out_shape=part_shapes + [shape((n, 128, 128), t) for n, t in zip(sizes, dtypes)],
        compiler_params=pltpu.CompilerParams(vmem_limit_bytes=30 * MIB),
        cost_estimate=pl.CostEstimate(flops=32 * 10**9, bytes_accessed=30 * 10**6, transcendentals=10**6),
        name="window_pass",
    )(scalars, *xs, *us, *ws)


def after(values, *earlier):
    return lax.optimization_barrier(tuple(values) + earlier)[:len(values)]


def local(tokens, upstream, qkv_weight, out_weight):
    lon = lax.axis_index("lon")
    lat = lax.axis_index("lat")
    xh, y, c = lon // 8, (lon // 2) % 4, lon % 2
    last = (lat == lax.axis_size("lat") - 1).astype(jnp.int32)
    scalars = jnp.stack([jnp.int32(v) for v in (xh, c, y, last)])

    split, out_blocks = weight_split(scalars, qkv_weight, out_weight)
    token_low = hop_z(tokens[:6], -1)
    (upstream,) = after((upstream,), out_blocks)
    from_x = swap_x(jnp.stack([split[2], split[3]]))
    next_cols = next_lon(upstream[:, :3])

    cols = jnp.concatenate([upstream[:, 3:], next_cols], axis=1)
    cols = cols.reshape(2, 6, 2, WLON, LEVELS, D).transpose(0, 2, 1, 3, 4, 5).reshape(2, 2, HALF, D)
    pieces = token_split(scalars, tokens, token_low)
    u_low, u_high, *pieces = after((cols[0], cols[1], *pieces))
    from_c = swap_c(jnp.stack([split[1], from_x[1]]))
    u_x = [swap_x(u_high)]
    u_low = hop_z(u_low, -1)
    pieces = [pieces[0]] + [shift_y(pieces[s], s) for s in (1, 2, 3)]
    x_high = jnp.stack([piece[0] for piece in pieces]).reshape(4, 2, 4, HALF, 128)
    x_low = jnp.stack([piece[1] for piece in pieces]).reshape(4, 2, 4, HALF, 128)

    shard = jnp.concatenate([split[0], from_x[0], from_c.reshape(12, 128, 128), out_blocks])
    shard, u_low, x_high, x_low = after((shard, u_low, x_high, x_low), from_c, u_low, u_x[0], *pieces[1:])
    w_up, w_down = shift_y(shard, 1), shift_y(shard, -1)
    u_x.append(across(u_low, True))
    u_own = [u_high, across(u_low, False)]
    highs = [x_high, swap_c(x_high), swap_x(x_high)]

    up_half, down_half, x_low = after(
        (w_up[:16], w_down[16:], x_low), w_up, w_down, u_x[1], u_own[1], highs[2])
    ws = [shard, w_up, shift_y(up_half, 1), w_down, shift_y(down_half, -1)]
    lows = [across(x_low, False), across(x_low, True)]
    u_own, u_x = (jnp.concatenate(u, axis=1) for u in (u_own, u_x))
    us = [u_own, swap_c(u_own), u_x]

    lows[0], lows[1], to_c, u_x = after((*lows, highs[2], u_x), ws[2], ws[4], highs[1], us[1])
    us.append(swap_c(u_x))
    highs.append(swap_c(to_c))
    lows = [lows[0], swap_c(lows[0]), lows[1], swap_c(lows[1])]

    xs = highs + lows
    part_c, part_x, part_own, lower, upper, up, down, mine = window_pass(scalars, xs, us, ws)

    def plus(a, b):
        return (a.astype(jnp.float32) + b.astype(jnp.float32)).astype(jnp.bfloat16)

    got_c = swap_c(part_c)
    own = part_own.astype(jnp.float32) + got_c[0].astype(jnp.float32)
    other = plus(part_x, got_c[1])

    lower, upper = shift_y(lower, -1), shift_y(upper, 1)
    low = [across(own[..., HALF:, :].astype(jnp.bfloat16), False), across(other[..., HALF:, :], True)]

    high, low = after((other[..., :HALF, :], plus(*low)), *low)
    up, down = after((plus(up, lower[:16]), plus(down, upper[16:])), lower, upper, high, low)
    high = (own[..., :HALF, :] + swap_x(high).astype(jnp.float32)).astype(jnp.bfloat16)
    low = hop_z(low, 1)
    up, down = shift_y(up, -1), shift_y(down, 1)

    total = mine.astype(jnp.float32) + jnp.concatenate([up, lower[16:]]).astype(jnp.float32) + jnp.concatenate(
        [upper[:16], down]).astype(jnp.float32)
    full = jnp.concatenate([high, low], axis=3)
    (total,) = after((total,), full)
    back = [full[0]] + [shift_y(full[s], -s) for s in (1, 2, 3)]
    blocks = total[:24].reshape(4, 6, 128, 128)
    sent = blocks.astype(jnp.bfloat16)
    by_x = swap_x(sent[2:])
    (near_x,) = after((by_x,), *back[1:])
    by_c = swap_c(jnp.stack([sent[1], near_x[1]]))
    grad_qkv_w = weight_join(scalars, total, by_c, by_x)
    grad_out_w = total[24:].reshape(8, 2, 64, 128).transpose(2, 0, 1, 3).reshape(64, D)

    result = token_join(scalars, [b.reshape(2, 4, WLAT, WLON, LEVELS, 128) for b in back])
    return (result, grad_qkv_w[None], grad_out_w[None])


def solution(mesh):
    return jax.shard_map(
        local,
        mesh=mesh,
        in_specs=(
            P("lat", None, None, "lon"),
            P("lat", "lon", None, None),
            P("lon", None),
            P("lon", None),
        ),
        out_specs=(P("lat", None, None, "lon"), P("lat", "lon", None), P("lat", "lon", None)),
        check_vma=False,
    )
```

```python
import functools

import jax
import jax.numpy as jnp
from jax import lax
from jax.experimental import pallas as pl
from jax.experimental.pallas import tpu as pltpu
from jax.sharding import PartitionSpec as P

HEAD_DIM = 64
WLAT = 12
WLON = 6
LEVELS = 2
WTOK = WLAT * WLON * LEVELS
PAIR = 2 * WTOK
HALF = WTOK // 2
D = 2048
NY = 4
MIB = 1024 * 1024

NEG_FILL = -1e30
EPSILON = 1e-05


def lon_of(xh, y, c):
    return (xh * NY + y) * 2 + c


COORDS = [(xh, y, c) for xh in range(2) for y in range(NY) for c in range(2)]


def swap_c(value):
    return lax.ppermute(value, "lon", [(lon_of(x, y, c), lon_of(x, y, 1 - c)) for x, y, c in COORDS])


def swap_x(value):
    return lax.ppermute(value, "lon", [(lon_of(x, y, c), lon_of(1 - x, y, c)) for x, y, c in COORDS])


def shift_y(value, by):
    return lax.ppermute(value, "lon", [(lon_of(x, y, c), lon_of(x, (y + by) % NY, c)) for x, y, c in COORDS])


def hop_z(value, by):
    rows, lons = lax.axis_size("lat"), lax.axis_size("lon")
    pairs = [
        (r * lons + i, (r + (2 * by if r % 2 == 0 else 0)) % rows * lons + i) for r in range(rows) for i in range(lons)
    ]
    return lax.ppermute(value, ("lat", "lon"), pairs)


def across(value, other):
    rows, lons = lax.axis_size("lat"), lax.axis_size("lon")
    pairs = [
        (r * lons + i, (r ^ 1) * lons + (lon_of(1 - i // 8, i // 2 % NY, i % 2) if other else i))
        for r in range(rows) for i in range(lons)
    ]
    return lax.ppermute(value, ("lat", "lon"), pairs)


def next_lon(value):
    return lax.ppermute(value, "lon", [(i, (i - 1) % 16) for i in range(16)])


def mm(a, b, dims):
    return lax.dot_general(a, b, (dims, ((), ())), preferred_element_type=jnp.float32)


def shape(dims, dtype=jnp.bfloat16):
    return jax.ShapeDtypeStruct(dims, dtype)


def whole(*dims):
    return pl.BlockSpec(dims, lambda *_: (0,) * len(dims))


def weight_split_kernel(s_ref, q_ref, o_ref, w_ref, out_ref):
    group = s_ref[0] * 2 + s_ref[1]
    for xh in range(2):
        for c in range(2):
            slot = group ^ (xh * 2 + c)
            for part in range(3):
                for pair in range(2):
                    lo = (part * 8 + xh * 4 + pair * 2) * 128 + c * 64
                    w_ref[slot, part * 2 + pair] = jnp.concatenate(
                        [q_ref[:, lo:lo + 64], q_ref[:, lo + 128:lo + 192]], axis=1)
    for i in range(8):
        out_ref[i] = jnp.concatenate(
            [o_ref[:, i * 256:i * 256 + 128], o_ref[:, i * 256 + 128:i * 256 + 256]], axis=0)


def weight_split(scalars, qkv_weight, out_weight):
    return pl.pallas_call(
        weight_split_kernel,
        grid_spec=pltpu.PrefetchScalarGridSpec(
            num_scalar_prefetch=1,
            grid=(1,),
            in_specs=[whole(128, 3072), whole(64, D)],
            out_specs=[whole(4, 6, 128, 128), whole(8, 128, 128)],
        ),
        out_shape=[shape((4, 6, 128, 128)), shape((8, 128, 128))],
        cost_estimate=pl.CostEstimate(flops=0, bytes_accessed=2 * 10**6, transcendentals=0),
        name="weight_split",
    )(scalars, qkv_weight, out_weight)


def weight_join_kernel(s_ref, a_ref, b_ref, c_ref, out_ref):
    group = s_ref[0] * 2 + s_ref[1]

    def block(slot, index):
        return jnp.where(slot == 0, a_ref[index], jnp.where(
            slot == 1, b_ref[0, index].astype(jnp.float32), jnp.where(
                slot == 3, b_ref[1, index], c_ref[0, index]).astype(jnp.float32)))

    for xh in range(2):
        slots = [group ^ (xh * 2), group ^ (xh * 2 + 1)]
        for part in range(3):
            for pair in range(2):
                left, right = (block(slot, part * 2 + pair) for slot in slots)
                lo = (part * 8 + xh * 4 + pair * 2) * 128
                out_ref[:, lo:lo + 128] = jnp.concatenate([left[:, :64], right[:, :64]], axis=1)
                out_ref[:, lo + 128:lo + 256] = jnp.concatenate([left[:, 64:], right[:, 64:]], axis=1)


def weight_join(scalars, own, by_c, by_x):
    return pl.pallas_call(
        weight_join_kernel,
        grid_spec=pltpu.PrefetchScalarGridSpec(
            num_scalar_prefetch=1,
            grid=(1,),
            in_specs=[whole(6, 128, 128), whole(2, 6, 128, 128), whole(2, 6, 128, 128)],
            out_specs=whole(128, 3072),
        ),
        out_shape=shape((128, 3072), jnp.float32),
        compiler_params=pltpu.CompilerParams(vmem_limit_bytes=60 * MIB),
        cost_estimate=pl.CostEstimate(flops=0, bytes_accessed=3 * 10**6, transcendentals=0),
        name="weight_join",
    )(scalars, own, by_c, by_x)


def spans(y):
    for s in range(4):
        for w in range(2):
            for t in range(4):
                xh, c = t // 2, t % 2
                start = 12 * lon_of(xh, lax.rem(y + s, 4), c) + 3 + 6 * w
                if xh == 1 and c == 1 and w == 1:
                    yield s, w, t, start, 0, 3
                    yield s, w, t, lax.rem(start + 3, 192), 3, 3
                else:
                    yield s, w, t, start, 0, 6


def token_split_kernel(s_ref, high_ref, low_ref, *outs):
    for s, w, t, start, offset, columns in spans(s_ref[2]):
        for half, ref in enumerate((high_ref, low_ref)):
            outs[s][half, w, t, :, offset:offset + columns] = ref[:, pl.ds(start, columns)]


def token_split(scalars, tokens, low):
    dims = (2, 2, 4, 6, WLON, LEVELS, 128)
    return pl.pallas_call(
        token_split_kernel,
        grid_spec=pltpu.PrefetchScalarGridSpec(
            num_scalar_prefetch=1,
            grid=(1,),
            in_specs=[
                pl.BlockSpec((6, 192, LEVELS, 128), lambda i, r: (1, 0, 0, 0)), whole(6, 192, LEVELS, 128),
            ],
            out_specs=[whole(*dims)] * 4,
        ),
        out_shape=[shape(dims)] * 4,
        compiler_params=pltpu.CompilerParams(vmem_limit_bytes=40 * MIB),
        cost_estimate=pl.CostEstimate(flops=0, bytes_accessed=3 * 10**6, transcendentals=0),
        name="token_split",
    )(scalars, tokens, low)


def token_join_kernel(s_ref, *refs):
    parts, out_ref = refs[:4], refs[4]
    for s, w, t, start, offset, columns in spans(s_ref[2]):
        out_ref[6:12, pl.ds(start, columns)] = parts[s][w, t, 0:6, offset:offset + columns]
        out_ref[0:6, pl.ds(start, columns)] = parts[s][w, t, 6:12, offset:offset + columns]


def token_join(scalars, parts):
    return pl.pallas_call(
        token_join_kernel,
        grid_spec=pltpu.PrefetchScalarGridSpec(
            num_scalar_prefetch=1,
            grid=(1,),
            in_specs=[whole(2, 4, WLAT, WLON, LEVELS, 128)] * 4,
            out_specs=whole(WLAT, 192, LEVELS, 128),
        ),
        out_shape=shape((WLAT, 192, LEVELS, 128)),
        compiler_params=pltpu.CompilerParams(vmem_limit_bytes=40 * MIB),
        cost_estimate=pl.CostEstimate(flops=0, bytes_accessed=3 * 10**6, transcendentals=0),
        name="token_join",
    )(scalars, *parts)


def attend(qkv, grad_att, split):
    scale = HEAD_DIM ** -0.5
    lane = lax.broadcasted_iota(jnp.int32, (1, 128), 1)
    row_group = lax.broadcasted_iota(jnp.int32, (WTOK, WTOK), 0) >= HALF
    col_group = lax.broadcasted_iota(jnp.int32, (WTOK, WTOK), 1) >= HALF
    keep = (row_group == col_group) | (split == 0)
    units = []
    for w in range(2):
        rows = slice(w * WTOK, (w + 1) * WTOK)
        for pair in range(2):
            cols = slice(pair * 128, (pair + 1) * 128)
            q = qkv[rows, 0:256][:, cols] * scale
            k = qkv[rows, 256:512][:, cols]
            v = qkv[rows, 512:768][:, cols]
            g = grad_att[rows, cols]
            heads = []
            for h in range(2):
                mine = (lane < 64) == (h == 0)
                heads.append((
                    jnp.where(mine, q, 0.0).astype(jnp.bfloat16),
                    jnp.where(mine, g, 0.0).astype(jnp.bfloat16),
                ))
            kb, vb = k.astype(jnp.bfloat16), v.astype(jnp.bfloat16)
            units.append((heads, kb, vb, k.T.astype(jnp.bfloat16), v.T.astype(jnp.bfloat16)))
    work = [(u, h) for u in range(4) for h in range(2)]
    scores = {
        (u, h): mm(units[u][1], units[u][0][h][0], ((1,), (1,))) for u, h in work
    }
    probs, probs_b = {}, {}
    for key in work:
        kept = jnp.where(keep, scores[key], NEG_FILL)
        expons = jnp.exp(kept - jnp.max(kept, axis=0, keepdims=True))
        probs[key] = expons * (1.0 / jnp.sum(expons, axis=0, keepdims=True))
        probs_b[key] = probs[key].astype(jnp.bfloat16)
    grads = {}
    for u, h in work:
        weighted = probs[u, h] * mm(units[u][2], units[u][0][h][1], ((1,), (1,)))
        inner = jnp.sum(weighted, axis=0, keepdims=True)
        grads[u, h] = (weighted - probs[u, h] * inner).astype(jnp.bfloat16)
    att, dq, dk, dv = [], [], [], []
    for u in range(4):
        heads, _, _, kt, vt = units[u]
        att.append(jnp.concatenate(
            [mm(vt[h * 64:(h + 1) * 64], probs_b[u, h], ((1,), (0,))) for h in range(2)], axis=0).T)
        dq.append(jnp.concatenate(
            [mm(kt[h * 64:(h + 1) * 64], grads[u, h], ((1,), (0,))) for h in range(2)], axis=0).T * scale)
        dk.append(sum(mm(grads[u, h], heads[h][0], ((1,), (0,))) for h in range(2)))
        dv.append(sum(mm(probs_b[u, h], heads[h][1], ((1,), (0,))) for h in range(2)))
    attended = jnp.concatenate([jnp.concatenate(att[2 * w:2 * w + 2], axis=1) for w in range(2)], axis=0)
    dqkv = jnp.concatenate([
        jnp.concatenate(dq[2 * w:2 * w + 2] + dk[2 * w:2 * w + 2] + dv[2 * w:2 * w + 2], axis=1)
        for w in range(2)], axis=0)
    return attended.astype(jnp.bfloat16), dqkv.astype(jnp.bfloat16)


ORDER = (2, 1, 3, 0)


def window_kernel(s_ref, *refs):
    highs, lows, us, ws = refs[:4], refs[4:8], refs[8:12], refs[12:17]
    pc_ref, px_ref, po_ref = refs[17:20]
    terms = refs[20:25]
    wfull, wout, ub, gacc, nb_all, dq_all, wsum, att_all = refs[25:]
    i = pl.program_id(0)
    c, y = s_ref[1], s_ref[2]

    @pl.when(i == 0)
    def _():
        for s in range(4):
            def block(index):
                if s == 2:
                    return ws[2][index] if index < 16 else ws[4][index - 16]
                return ws[s][index]
            for k in range(4):
                row = (s * 4 + k) * 128
                for part in range(6):
                    wfull[row:row + 128, part * 128:(part + 1) * 128] = block((0, 2, 1, 3)[k] * 6 + part)
            head = lax.rem(y + 4 - s, 4)
            rows = pl.ds(pl.multiple_of(head * 64, 64), 64)
            for j in range(8):
                wout[rows, j * 256:j * 256 + 128] = block(24 + j)[0:64]
                wout[rows, j * 256 + 128:j * 256 + 256] = block(24 + j)[64:128]
        wsum[...] = jnp.sum(wfull[...].astype(jnp.float32), axis=0, keepdims=True)

    rows = pl.ds(pl.multiple_of(i * PAIR, PAIR), PAIR)
    for step in range(4):
        @pl.when(i == step)
        def _():
            for dc in range(2):
                ub[pl.ds(pl.multiple_of(step * PAIR + (dc ^ c) * WTOK, WTOK), WTOK), :] = us[2 * (step % 2) + dc][0]

    x = jnp.concatenate([
        jnp.concatenate(
            [half[k][s, 0].astype(jnp.float32) for half in (highs, lows)], axis=1).reshape(PAIR, 128)
        for s in range(4) for k in range(4)
    ], axis=1)
    centred = x - jnp.mean(x, axis=-1, keepdims=True)
    inverse = lax.rsqrt(jnp.mean(centred * centred, axis=-1, keepdims=True) + EPSILON)
    nb = (centred * inverse).astype(jnp.bfloat16)
    nb_all[rows, :] = nb
    qkv = mm(nb, wfull[...], ((1,), (0,)))
    grad_att = mm(ub[rows, :], wout[...], ((1,), (1,)))
    attended, dqkv = attend(qkv, grad_att, s_ref[3])
    att_all[rows, :] = attended
    dq_all[rows, :] = dqkv
    dqkv_f = dqkv.astype(jnp.float32)
    mean_one = jnp.sum(dqkv_f * wsum[...], axis=-1, keepdims=True) * (inverse / D)
    mean_two = jnp.sum(dqkv_f * qkv, axis=-1, keepdims=True) * (inverse / D)
    grad_normal = mm(dqkv, wfull[...], ((1,), (1,)))
    normal = nb_all[rows, :].astype(jnp.float32)
    grad_rolled = inverse * grad_normal - mean_one - normal * mean_two

    for s in range(4):
        part = [grad_rolled[:, (s * 4 + k) * 128:(s * 4 + k + 1) * 128].reshape(2, WTOK, 128) for k in range(4)]
        pc_ref[0, s, 0] = part[1].astype(jnp.bfloat16)
        pc_ref[1, s, 0] = part[3].astype(jnp.bfloat16)
        px_ref[s, 0] = part[2].astype(jnp.bfloat16)
        block = lon_of(s_ref[0], lax.rem(y + 4 - s, 4), c)
        own = ub[rows, pl.ds(pl.multiple_of(block * 128, 128), 128)].astype(jnp.float32)
        po_ref[s, 0] = (part[0] + own.reshape(2, WTOK, 128)).astype(jnp.bfloat16)

    @pl.when(i == 3)
    def _():
        gacc[...] = mm(att_all[...], ub[...], ((0,), (0,)))
        for step, s in enumerate(ORDER):
            def put(index, value):
                if s == 2:
                    at, place = (0, index) if index < 16 else (1, index - 4)
                elif s == 1:
                    at, place = (2, index) if index < 20 else (0, index - 4)
                elif s == 3:
                    at, place = (1, index) if index < 12 else (3, index - 12)
                else:
                    at, place = 4, index
                terms[at][place] = value.astype(jnp.bfloat16)

            term = mm(nb_all[:, s * 512:(s + 1) * 512], dq_all[...], ((0,), (0,)))
            for k in range(4):
                for part in range(6):
                    put(k * 6 + part, term[k * 128:(k + 1) * 128, part * 128:(part + 1) * 128])
            head = lax.rem(y + 4 - s, 4)
            gw = gacc[pl.ds(pl.multiple_of(head * 64, 64), 64), :]
            for j in range(8):
                put(24 + j, jnp.concatenate(
                    [gw[:, j * 256:j * 256 + 128], gw[:, j * 256 + 128:j * 256 + 256]], axis=0))


def once(*dims):
    return pl.BlockSpec(dims, lambda *_: (0,) * len(dims), pipeline_mode=pl.Buffered(1))


def window_pass(scalars, xs, us, ws):
    sizes = [28, 28, 20, 20, 32]
    dtypes = [jnp.bfloat16] * 5
    tile = pl.BlockSpec((4, 1, 2, WTOK, 128), lambda i, s: (0, i // 2, (i % 2) ^ s[0], 0, 0))
    part_specs = [
        pl.BlockSpec((2, 4, 1, 2, WTOK, 128), lambda i, s: (0, 0, i // 2, (i % 2) ^ s[0], 0, 0)), tile, tile,
    ]
    part_shapes = [
        shape((2, 4, 2, 4, WTOK, 128)), shape((4, 2, 4, WTOK, 128)), shape((4, 2, 4, WTOK, 128)),
    ]
    return pl.pallas_call(
        window_kernel,
        grid_spec=pltpu.PrefetchScalarGridSpec(
            num_scalar_prefetch=1,
            grid=(4,),
            in_specs=[
                pl.BlockSpec((4, 1, 2, HALF, 128), lambda i, s: (0, i // 2, (i % 2) ^ s[0], 0, 0))
            ] * 8 + [pl.BlockSpec((1, WTOK, D), lambda i, s: (i // 2, 0, 0))] * 4
            + [once(n, 128, 128) for n in (32, 32, 16, 32, 16)],
            out_specs=part_specs + [once(n, 128, 128) for n in sizes],
            scratch_shapes=[
                pltpu.VMEM((D, 768), jnp.bfloat16),
                pltpu.VMEM((256, D), jnp.bfloat16),
                pltpu.VMEM((4 * PAIR, D), jnp.bfloat16),
                pltpu.VMEM((256, D), jnp.float32),
                pltpu.VMEM((4 * PAIR, D), jnp.bfloat16),
                pltpu.VMEM((4 * PAIR, 768), jnp.bfloat16),
                pltpu.VMEM((1, 768), jnp.float32),
                pltpu.VMEM((4 * PAIR, 256), jnp.bfloat16),
            ],
        ),
        out_shape=part_shapes + [shape((n, 128, 128), t) for n, t in zip(sizes, dtypes)],
        compiler_params=pltpu.CompilerParams(vmem_limit_bytes=30 * MIB),
        cost_estimate=pl.CostEstimate(flops=32 * 10**9, bytes_accessed=30 * 10**6, transcendentals=10**6),
        name="window_pass",
    )(scalars, *xs, *us, *ws)


def after(values, *earlier):
    return lax.optimization_barrier(tuple(values) + earlier)[:len(values)]


def local(tokens, upstream, qkv_weight, out_weight):
    lon = lax.axis_index("lon")
    lat = lax.axis_index("lat")
    xh, y, c = lon // 8, (lon // 2) % 4, lon % 2
    last = (lat == lax.axis_size("lat") - 1).astype(jnp.int32)
    scalars = jnp.stack([jnp.int32(v) for v in (xh, c, y, last)])

    split, out_blocks = weight_split(scalars, qkv_weight, out_weight)
    token_low = hop_z(tokens[:6], -1)
    (upstream,) = after((upstream,), out_blocks)
    from_x = swap_x(jnp.stack([split[2], split[3]]))
    next_cols = next_lon(upstream[:, :3])

    cols = jnp.concatenate([upstream[:, 3:], next_cols], axis=1)
    cols = cols.reshape(2, 6, 2, WLON, LEVELS, D).transpose(0, 2, 1, 3, 4, 5).reshape(2, 2, HALF, D)
    pieces = token_split(scalars, tokens, token_low)
    u_low, u_high, *pieces = after((cols[0], cols[1], *pieces))
    from_c = swap_c(jnp.stack([split[1], from_x[1]]))
    u_x = [swap_x(u_high)]
    u_low = hop_z(u_low, -1)
    pieces = [pieces[0]] + [shift_y(pieces[s], s) for s in (1, 2, 3)]
    x_high = jnp.stack([piece[0] for piece in pieces]).reshape(4, 2, 4, HALF, 128)
    x_low = jnp.stack([piece[1] for piece in pieces]).reshape(4, 2, 4, HALF, 128)

    shard = jnp.concatenate([split[0], from_x[0], from_c.reshape(12, 128, 128), out_blocks])
    shard, u_low, x_high, x_low = after((shard, u_low, x_high, x_low), from_c, u_low, u_x[0], *pieces[1:])
    w_up, w_down = shift_y(shard, 1), shift_y(shard, -1)
    u_x.append(across(u_low, True))
    u_own = [u_high, across(u_low, False)]
    highs = [x_high, swap_c(x_high), swap_x(x_high)]

    up_half, down_half, x_low = after(
        (w_up[:16], w_down[16:], x_low), w_up, w_down, u_x[1], u_own[1], highs[2])
    ws = [shard, w_up, shift_y(up_half, 1), w_down, shift_y(down_half, -1)]
    lows = [across(x_low, False), across(x_low, True)]
    u_own, u_x = (jnp.concatenate(u, axis=1) for u in (u_own, u_x))
    us = [u_own, swap_c(u_own), u_x]

    lows[0], lows[1], to_c, u_x = after((*lows, highs[2], u_x), ws[2], ws[4], highs[1], us[1])
    us.append(swap_c(u_x))
    highs.append(swap_c(to_c))
    lows = [lows[0], swap_c(lows[0]), lows[1], swap_c(lows[1])]

    xs = highs + lows
    part_c, part_x, part_own, lower, upper, up, down, mine = window_pass(scalars, xs, us, ws)

    def plus(a, b):
        return (a.astype(jnp.float32) + b.astype(jnp.float32)).astype(jnp.bfloat16)

    got_c = swap_c(part_c)
    own = part_own.astype(jnp.float32) + got_c[0].astype(jnp.float32)
    other = plus(part_x, got_c[1])

    lower, upper = shift_y(lower, -1), shift_y(upper, 1)
    low = [across(own[..., HALF:, :].astype(jnp.bfloat16), False), across(other[..., HALF:, :], True)]

    high, low = after((other[..., :HALF, :], plus(*low)), *low)
    up = jnp.concatenate([plus(up[:16], lower[:16]), up[16:]])
    down = jnp.concatenate([down[:4], plus(down[4:], upper[12:])])
    up, down = after((up, down), lower, upper, high, low)
    high = (own[..., :HALF, :] + swap_x(high).astype(jnp.float32)).astype(jnp.bfloat16)
    low = hop_z(low, 1)
    up, down = shift_y(up, -1), shift_y(down, 1)

    total = mine.astype(jnp.float32) + jnp.concatenate([up, lower[16:]]).astype(jnp.float32) + jnp.concatenate(
        [upper[:12], down]).astype(jnp.float32)
    full = jnp.concatenate([high, low], axis=3)
    (total,) = after((total,), full)
    back = [full[0]] + [shift_y(full[s], -s) for s in (1, 2, 3)]
    blocks = total[:24].reshape(4, 6, 128, 128)
    sent = blocks.astype(jnp.bfloat16)
    by_x = swap_x(sent[2:])
    (near_x,) = after((by_x,), *back[1:])
    by_c = swap_c(jnp.stack([sent[1], near_x[1]]))
    grad_qkv_w = weight_join(scalars, total, by_c, by_x)
    grad_out_w = total[24:].reshape(8, 2, 64, 128).transpose(2, 0, 1, 3).reshape(64, D)

    result = token_join(scalars, [b.reshape(2, 4, WLAT, WLON, LEVELS, 128) for b in back])
    return (result, grad_qkv_w[None], grad_out_w[None])


def solution(mesh):
    return jax.shard_map(
        local,
        mesh=mesh,
        in_specs=(
            P("lat", None, None, "lon"),
            P("lat", "lon", None, None),
            P("lon", None),
            P("lon", None),
        ),
        out_specs=(P("lat", None, None, "lon"), P("lat", "lon", None), P("lat", "lon", None)),
        check_vma=False,
    )
```
